256 devices in a mesh: rep: 2 (over core), dp: 16 (over y_lo, z), tensor: 8 (over x, y_hi).
Axes of the slice: x: 4, y: 4 (y_hi: 2, y_lo: 2; y = y_hi * 2 + y_lo), z: 8, core: 2. Of those that a mesh axis runs over, the one named last changes fastest.
Arguments:
- hidden_in: bfloat16 [16384, 8192], P(('rep', 'dp', 'tensor')), may hold values from -24 to 24
- queries: bfloat16 [16384, 8192], P(('rep', 'dp'), 'tensor'), may hold values from -6 to 6
- keys: bfloat16 [16384, 1024], P(('rep', 'dp'), 'tensor'), may hold values from -6 to 6
- values: bfloat16 [16384, 1024], P(('rep', 'dp'), 'tensor'), may hold values from -6 to 6
- out_grad: bfloat16 [16384, 8192], P(('rep', 'dp'), 'tensor'), may hold values from -6 to 6
- w_key: bfloat16 [8192, 1024], P('dp', 'tensor'), may hold values from -0.0625 to 0.0625
- w_value: bfloat16 [8192, 1024], P('dp', 'tensor'), may hold values from -0.0625 to 0.0625
- adam_state: float32 [2, 2, 8192, 1024], P(None, None, ('rep', 'dp'), 'tensor'), may hold values from -6 to 6
Outputs:
- query_grad: bfloat16 [16384, 8192], P(('rep', 'dp'), 'tensor')
- input_grad: bfloat16 [16384, 8192], P(('rep', 'dp', 'tensor'))
- key_weight_grad: float32 [8192, 1024], P(('rep', 'dp'), 'tensor')
- value_weight_grad: float32 [8192, 1024], P(('rep', 'dp'), 'tensor')
- state_backup: float32 [2, 2, 8192, 1024], P(None, None, ('rep', 'dp'), 'tensor')
The draws below stay inside these ranges and needn't reach their ends.
All inputs are finite; a program needn't handle non-finite values.
Results may differ from the reference program's by a relative error of at most 0.015.
Values may be sent and summed in bfloat16 or wider, within the bound.
No kernel may reach another device: no remote copies, remote signals or barrier semaphores. Data moves between devices by JAX's collectives and lax.ppermute only.
A program may use at most 128 MiB of HBM per device.

```python
import math
import jax
import jax.numpy as jnp
from jax import lax

D = 8192
HEADS = 64
KVH = 8
HD = 128
LEN = 512
TOKENS = 16384
QW = 8192
KVW = 1024
N_TENSOR = 8


def draw_keys(key, part):
    key = jax.random.fold_in(key, 11)
    return jax.random.truncated_normal(key, -6.0, 6.0, (TOKENS, KVW), jnp.float32).astype(jnp.bfloat16)


def draw_queries(key, part):
    key = jax.random.fold_in(key, 12)
    return jax.random.truncated_normal(key, -6.0, 6.0, (TOKENS, QW), jnp.float32).astype(jnp.bfloat16)


def with_spikes(entries, rng, source, target, parts, factor):
    owner, partner = [(jnp.arange(entries.shape[axis_at]) // (entries.shape[axis_at] // parts)).reshape([-1 if axis == axis_at else 1 for axis in range(entries.ndim)]) for axis_at in (source, target)]
    chosen = jax.random.permutation(rng, parts)[partner]
    strong = (owner == chosen) | (owner == (partner + parts // 2) % parts)
    return jnp.where(strong, factor * entries, entries)


def shard_levels(stream_key, shape, split, smallest, top_value):
    factor_of, own = 1.0, jax.random.fold_in(stream_key, 6)
    for axis_at, blocks in split:
        steps = jnp.exp(jax.random.uniform(jax.random.fold_in(own, axis_at), (blocks,), jnp.float32, smallest / len(split), top_value / len(split)))
        factor_of = factor_of * jnp.repeat(steps, shape[axis_at] // blocks).reshape([-1 if axis == axis_at else 1 for axis in range(len(shape))])
    return factor_of


def scatter_about(key, dims, spread, bound, split=(), held_as=jnp.bfloat16):
    loudness = shard_levels(key, dims, split, -0.22, 0.18) if split else 1.0
    result = jax.random.normal(key, dims, jnp.float32) * spread * loudness
    return jnp.minimum(jnp.maximum(result, -bound), bound).astype(held_as)


def bell_draw_with(stream_key, dims, spread, limit, shards, heavy, dtype=jnp.bfloat16):
    result = spread * jax.random.normal(stream_key, dims, jnp.float32)
    if shards:
        result = result * shard_levels(stream_key, dims, shards, -0.22, 0.18)
    return jnp.clip(with_spikes(result, jax.random.fold_in(stream_key, 3), *heavy), -limit, limit).astype(dtype)


def setup_inputs(seed: int = 0) -> dict:
    key_of = jax.random.split(jax.random.key(seed), 9)
    hidden_in = bell_draw_with(key_of[0], (TOKENS, D), 1.0, 24.0, ((0, 256),), (0, 1, 256, 6.0))
    queries = draw_queries(jax.random.fold_in(key_of[8], 71), 0)
    keys = draw_keys(jax.random.fold_in(key_of[8], 71), 0)
    values = scatter_about(key_of[3], (TOKENS, KVW), 1.0, 6.0, ((0, 32), (1, 8)))
    out_grad = scatter_about(key_of[4], (TOKENS, QW), 1.0, 6.0, ((0, 32), (1, 8)))
    w_key = scatter_about(key_of[5], (D, KVW), D ** -0.5, 0.0625, ((0, 16), (1, 8)))
    w_value = scatter_about(key_of[6], (D, KVW), D ** -0.5, 0.0625, ((0, 16), (1, 8)))
    adam_state = scatter_about(key_of[7], (2, 2, D, KVW), 1.0, 6.0, ((2, 32), (3, 8)), jnp.float32)
    return dict(hidden_in=hidden_in, queries=queries, keys=keys, values=values, out_grad=out_grad, w_key=w_key, w_value=w_value, adam_state=adam_state)


def rope_tables(seq_len):
    positions = jnp.arange(seq_len).astype(jnp.float32)
    half_dim = HD // 2
    exponents = jnp.arange(half_dim).astype(jnp.float32) * (2.0 / HD)
    frequency = jnp.exp(-math.log(1000000.0) * exponents)
    angles = positions[:, None] * frequency[None, :]
    return (jnp.cos(angles), jnp.sin(angles))

def unrotate(gradient, cosine, sine_table):
    half_dim = HD // 2
    first_half = gradient[..., :half_dim]
    second_half = gradient[..., half_dim:]
    cos_wide = cosine[:, None, :]
    sin_wide = sine_table[:, None, :]
    return jnp.concatenate([first_half * cos_wide + second_half * sin_wide, second_half * cos_wide - first_half * sin_wide], axis=-1)

def sequence_grads(operands):
    query_seq, key_seq, value_seq, grad_seq = operands
    per_group = HEADS // KVH
    softmax_scale = 1.0 / math.sqrt(HD)
    high = lax.Precision.HIGHEST
    query_heads = query_seq.astype(jnp.float32).reshape(LEN, KVH, per_group, HD)
    grad_heads = grad_seq.astype(jnp.float32).reshape(LEN, KVH, per_group, HD)
    key_heads = key_seq.astype(jnp.float32).reshape(LEN, KVH, HD)
    value_heads = value_seq.astype(jnp.float32).reshape(LEN, KVH, HD)
    scores = jnp.einsum('qkgd,pkd->kgqp', query_heads, key_heads, precision=high) * softmax_scale
    positions = jnp.arange(LEN)
    allowed = positions[None, :] <= positions[:, None]
    scores = jnp.where(allowed, scores, -jnp.inf)
    row_top = lax.optimization_barrier(jnp.max(scores, axis=-1, keepdims=True))
    weights = jnp.exp(scores - row_top)
    probabilities = weights / lax.optimization_barrier(jnp.sum(weights, axis=-1, keepdims=True))
    probs_low = probabilities.astype(jnp.bfloat16).astype(jnp.float32)
    dprobs = jnp.einsum('qkgd,pkd->kgqp', grad_heads, value_heads, precision=high)
    delta = lax.optimization_barrier(jnp.sum(probabilities * dprobs, axis=-1, keepdims=True))
    dscores = (probabilities * (dprobs - delta) * softmax_scale).astype(jnp.bfloat16).astype(jnp.float32)
    query_grad = jnp.einsum('kgqp,pkd->qkgd', dscores, key_heads, precision=high)
    rotated = jnp.einsum('kgqp,qkgd->pkd', dscores, query_heads, precision=high)
    value_grad = jnp.einsum('kgqp,qkgd->pkd', probs_low, grad_heads, precision=high)
    cosine, sine_table = rope_tables(LEN)
    key_grad = unrotate(rotated, cosine, sine_table)
    return (query_grad.reshape(LEN, QW).astype(jnp.bfloat16), key_grad.reshape(LEN, KVW).astype(jnp.bfloat16), value_grad.reshape(LEN, KVW).astype(jnp.bfloat16))

def reference(hidden_in, queries, keys, values, out_grad, w_key, w_value, adam_state):
    seq_count = TOKENS // LEN
    operands = (queries.reshape(seq_count, LEN, QW), keys.reshape(seq_count, LEN, KVW), values.reshape(seq_count, LEN, KVW), out_grad.reshape(seq_count, LEN, QW))
    query_grad, key_grad, value_grad = lax.map(sequence_grads, operands)
    key_flat = key_grad.reshape(TOKENS, KVW)
    value_flat = value_grad.reshape(TOKENS, KVW)
    key_weight_grad = jnp.dot(hidden_in.T, key_flat, preferred_element_type=jnp.float32)
    value_weight_grad = jnp.dot(hidden_in.T, value_flat, preferred_element_type=jnp.float32)
    group_width = KVW // N_TENSOR

    def input_rows(pair):
        key_rows, value_rows = pair
        total = jnp.zeros((LEN, D), jnp.float32)
        for group_index in range(N_TENSOR):
            lower = group_index * group_width
            upper = lower + group_width
            term = jnp.dot(key_rows[:, lower:upper], w_key[:, lower:upper].T, preferred_element_type=jnp.float32)
            term = term + jnp.dot(value_rows[:, lower:upper], w_value[:, lower:upper].T, preferred_element_type=jnp.float32)
            total = total + lax.optimization_barrier(term.astype(jnp.bfloat16)).astype(jnp.float32)
        return total.astype(jnp.bfloat16)
    input_grad = lax.map(input_rows, (key_grad, value_grad)).reshape(TOKENS, D)
    half_rows = D // 2
    state_backup = jnp.concatenate([adam_state[:, :, half_rows:], adam_state[:, :, :half_rows]], axis=2)
    return (query_grad.reshape(TOKENS, QW), input_grad, key_weight_grad, value_weight_grad, state_backup)
```

```python
import math

import jax
import jax.numpy as jnp
from jax import lax
from jax.sharding import Mesh
from jax.sharding import PartitionSpec as P

HEADS = 64
KVH = 8
HD = 128
REP, YLO, Z, TEN = 2, 2, 8, 8
PLANE = ("ylo", "tensor")


def shift(block, axis, count, by):
    return lax.ppermute(block, axis, [(i, (i + by) % count) for i in range(count)])


def rope_tables(seq_len):
    positions = jnp.arange(seq_len).astype(jnp.float32)
    half_dim = HD // 2
    exponents = jnp.arange(half_dim).astype(jnp.float32) * (2.0 / HD)
    frequency = jnp.exp(-math.log(1000000.0) * exponents)
    angles = positions[:, None] * frequency[None, :]
    return (jnp.cos(angles), jnp.sin(angles))


def unrotate(gradient, cosine, sine_table):
    half_dim = HD // 2
    first_half = gradient[..., :half_dim]
    second_half = gradient[..., half_dim:]
    return jnp.concatenate(
        [
            first_half * cosine + second_half * sine_table,
            second_half * cosine - first_half * sine_table,
        ],
        axis=-1,
    )


def attention_grads(queries, keys, values, out_grad):
    seq_len = queries.shape[0]
    per_group = HEADS // KVH
    softmax_scale = 1.0 / math.sqrt(HD)
    query_heads = queries.reshape(seq_len, per_group, HD)
    grad_heads = out_grad.reshape(seq_len, per_group, HD)
    positions = jnp.arange(seq_len)
    f32 = dict(preferred_element_type=jnp.float32)
    scores = jnp.einsum("qgd,pd->gqp", query_heads, keys, **f32) * softmax_scale
    allowed = positions[None, :] <= positions[:, None]
    scores = jnp.where(allowed, scores, -jnp.inf)
    row_top = jnp.max(scores, axis=-1, keepdims=True)
    weights = jnp.exp(scores - row_top)
    probabilities = weights / jnp.sum(weights, axis=-1, keepdims=True)
    probs_low = probabilities.astype(jnp.bfloat16)
    dprobs = jnp.einsum("qgd,pd->gqp", grad_heads, values, **f32)
    delta = jnp.sum(probabilities * dprobs, axis=-1, keepdims=True)
    dscores = (probabilities * (dprobs - delta) * softmax_scale).astype(jnp.bfloat16)
    query_grad = jnp.einsum("gqp,pd->qgd", dscores, keys, **f32)
    key_total = jnp.einsum("gqp,qgd->pd", dscores, query_heads, **f32)
    value_total = jnp.einsum("gqp,qgd->pd", probs_low, grad_heads, **f32)
    cosine, sine_table = rope_tables(seq_len)
    key_grad = unrotate(key_total, cosine, sine_table).astype(jnp.bfloat16)
    query_grad = query_grad.reshape(seq_len, per_group * HD).astype(jnp.bfloat16)
    return query_grad, key_grad, value_total.astype(jnp.bfloat16)


def ring_gather(block):
    up, down = [block], [block]
    half = block.shape[0] // 2
    for _ in range(Z // 2 - 1):
        up.append(shift(up[-1], "z", Z, 1))
        down.append(shift(down[-1], "z", Z, -1))
    far = jnp.concatenate([shift(up[-1][:half], "z", Z, 1), shift(down[-1][half:], "z", Z, -1)])
    return jnp.stack(down + [far] + up[:0:-1])


def on_device(hidden_in, queries, keys, values, out_grad, w_key, w_value, adam_state):
    rep, z = lax.axis_index("rep"), lax.axis_index("z")
    first = rep == 0
    state_backup = shift(adam_state, "rep", REP, 1)
    rows, width = hidden_in.shape
    out_rows = width // (REP * YLO * Z)
    w_rows = width // (YLO * Z)

    hidden = hidden_in.reshape(rows, REP * YLO, Z, out_rows).transpose(2, 0, 1, 3)
    hidden = lax.all_to_all(hidden, "z", split_axis=0, concat_axis=0, tiled=True)
    hidden = lax.dynamic_slice_in_dim(jnp.concatenate([hidden, hidden]), z, Z)
    hidden = hidden.reshape(Z * rows, REP * YLO * out_rows)
    hidden = jnp.concatenate([hidden, shift(hidden, "rep", REP, 1)])

    weight = jnp.where(first, w_key, w_value)
    weight = jnp.broadcast_to(weight[None], (YLO * TEN,) + weight.shape)
    weight = lax.all_to_all(weight, PLANE, split_axis=0, concat_axis=0, tiled=True)
    weight = weight.reshape(YLO, TEN, w_rows, HD).transpose(0, 2, 1, 3)
    weight = weight.reshape(YLO * w_rows, TEN * HD)

    query_grad, key_grad, value_grad = attention_grads(queries, keys, values, out_grad)

    own = jnp.where(first, key_grad, value_grad)
    other = shift(jnp.where(first, value_grad, key_grad), "rep", REP, 1)
    grads = jnp.stack([own, other]).reshape(REP, TEN, rows, HD).transpose(1, 0, 2, 3)
    grads = lax.all_to_all(grads, "tensor", split_axis=0, concat_axis=0, tiled=True)
    grads = grads.transpose(1, 2, 0, 3).reshape(REP * rows, TEN * HD)
    grads = ring_gather(grads).reshape(Z, REP, rows, TEN * HD).transpose(1, 0, 2, 3)
    grads = grads.reshape(REP * Z * rows, TEN * HD)

    partial = lax.dot_general(
        hidden, grads, (((0,), (0,)), ((), ())), preferred_element_type=jnp.float32
    ).astype(jnp.bfloat16)
    partial = partial.reshape(REP, YLO, out_rows, TEN, HD).transpose(1, 3, 0, 2, 4)
    partial = partial.reshape(YLO * TEN, REP, out_rows, HD)
    partial = lax.all_to_all(partial, PLANE, split_axis=0, concat_axis=0, tiled=True)
    total = jnp.sum(partial.astype(jnp.float32), axis=0)
    kept = jnp.where(first, total[0], total[1])
    given = shift(jnp.where(first, total[1], total[0]), "rep", REP, 1)
    key_weight_grad = jnp.where(first, kept, given)
    value_weight_grad = jnp.where(first, given, kept)

    term = lax.dot_general(
        grads, weight, (((1,), (1,)), ((), ())), preferred_element_type=jnp.float32
    )
    half = Z * rows
    term = term[:half] + shift(term[half:].astype(jnp.bfloat16), "rep", REP, 1)
    term = term.astype(jnp.bfloat16).reshape(Z, rows, YLO, w_rows)
    arrived = [term[0]] + [shift(term[k], "z", Z, k) for k in range(1, Z)]
    arrived = jnp.stack(arrived[:1] + arrived[:0:-1])
    arrived = lax.dynamic_slice_in_dim(jnp.concatenate([arrived, arrived]), (Z - z) % Z, Z)
    input_grad = arrived.transpose(1, 2, 0, 3).reshape(rows, width)
    return (query_grad, input_grad, key_weight_grad, value_weight_grad, state_backup)


def solution(mesh):
    fine = Mesh(mesh.devices.reshape(REP, YLO, Z, TEN), ("rep", "ylo", "z", "tensor"))
    seqs = ("rep", "ylo", "z")
    return jax.shard_map(
        on_device,
        mesh=fine,
        in_specs=(
            P(seqs + ("tensor",), None),
            P(seqs, "tensor"),
            P(seqs, "tensor"),
            P(seqs, "tensor"),
            P(seqs, "tensor"),
            P(("ylo", "z"), "tensor"),
            P(("ylo", "z"), "tensor"),
            P(None, None, seqs, "tensor"),
        ),
        out_specs=(
            P(seqs, "tensor"),
            P(seqs + ("tensor",), None),
            P(seqs, "tensor"),
            P(seqs, "tensor"),
            P(None, None, seqs, "tensor"),
        ),
        check_vma=False,
    )
```

```python
import math

import jax
import jax.numpy as jnp
import numpy as np
from jax import lax
from jax.experimental import pallas as pl
from jax.experimental.pallas import tpu as pltpu
from jax.sharding import Mesh
from jax.sharding import PartitionSpec as P

HEADS = 64
KVH = 8
HD = 128
GROUP = HEADS // KVH
LEN = 512
REP, YLO, Z, TEN = 2, 2, 8, 8
PLANE = ("ylo", "tensor")
SCALE = 1.0 / math.sqrt(HD)
QB = 256
STEP_HEADS = 2
BF, F32 = jnp.bfloat16, jnp.float32

VMEM = pl.BlockSpec(memory_space=pltpu.VMEM)
SMEM = pl.BlockSpec(memory_space=pltpu.SMEM)
ANY = pl.BlockSpec(memory_space=pl.ANY)


def dot(a, b, ca, cb):
    return lax.dot_general(a, b, (((ca,), (cb,)), ((), ())), preferred_element_type=F32)


def struct(*shape, dtype=BF):
    return jax.ShapeDtypeStruct(shape, dtype)


def params(mib):
    return pltpu.CompilerParams(vmem_limit_bytes=mib * 2**20)


def cost(flops, nbytes):
    return pl.CostEstimate(flops=flops, bytes_accessed=nbytes, transcendentals=0)


def shift(block, axis, count, by):
    return lax.ppermute(block, axis, [(i, (i + by) % count) for i in range(count)])


def rope_wide():
    half = HD // 2
    angle = np.arange(LEN)[:, None] * 1000000.0 ** (-2.0 * np.arange(half) / HD)[None, :]
    cosine, sine = np.cos(angle), np.sin(angle)
    wide = np.concatenate([cosine, cosine], 1), np.concatenate([sine, -sine], 1)
    return [jnp.asarray(t.astype(np.float32)) for t in wide]


def attention_kernel(at_ref, q_ref, k_ref, v_ref, g_ref, c_ref, s_ref, _, qg_ref, own_ref, other_ref, kt, dk, dv):
    step = pl.program_id(0)

    @pl.when(step == 0)
    def _():
        kt[...] = k_ref[...].T
        dk[...] = jnp.zeros_like(dk)
        dv[...] = jnp.zeros_like(dv)

    key_at = lax.broadcasted_iota(jnp.int32, (QB, QB), 0)
    query_at = lax.broadcasted_iota(jnp.int32, (QB, QB), 1)
    allowed = key_at <= query_at
    for h in range(STEP_HEADS):
        lanes = slice(h * HD, (h + 1) * HD)
        for block in range(LEN // QB):
            rows = slice(block * QB, (block + 1) * QB)
            span = (block + 1) * QB
            q, g = q_ref[rows, lanes], g_ref[rows, lanes]
            scores = dot(k_ref[:span, :], q, 1, 1)
            scores = [scores[i * QB : (i + 1) * QB] for i in range(block + 1)]
            scores[-1] = jnp.where(allowed, scores[-1], -jnp.inf)
            scores = jnp.concatenate(scores, axis=0)
            top = jnp.max(scores, axis=0, keepdims=True)
            weights = jnp.exp2((scores - top) * (SCALE * math.log2(math.e)))
            inverse = 1.0 / jnp.sum(weights, axis=0, keepdims=True)
            probs = weights * inverse
            dprobs = dot(v_ref[:span, :], g, 1, 1)
            delta = jnp.sum(probs * dprobs, axis=0, keepdims=True)
            dscores = (probs * ((dprobs - delta) * SCALE)).astype(BF)
            dk[:span, :] += dot(dscores, q, 1, 0)
            dv[:span, :] += dot(probs.astype(BF), g, 1, 0)
            qg_ref[rows, lanes] = dot(kt[:, :span], dscores, 1, 0).T.astype(BF)

    @pl.when(step == GROUP // STEP_HEADS - 1)
    def _():
        rotated = dk[...]
        turned = pltpu.roll(rotated, HD // 2, 1)
        key_grad = (rotated * c_ref[...] + turned * s_ref[...]).astype(BF)
        value_grad = dv[...].astype(BF)

        @pl.when(at_ref[0] == 0)
        def _():
            own_ref[...] = key_grad
            other_ref[...] = value_grad

        @pl.when(at_ref[0] != 0)
        def _():
            own_ref[...] = value_grad
            other_ref[...] = key_grad


def attention_grads(where_at, queries, keys, values, out_grad, before):
    whole = pl.BlockSpec((LEN, HD), lambda h: (0, 0))
    head = pl.BlockSpec((LEN, STEP_HEADS * HD), lambda h: (0, h))
    return pl.pallas_call(
        attention_kernel,
        grid=(GROUP // STEP_HEADS,),
        in_specs=[SMEM, head, whole, whole, head, whole, whole, ANY],
        out_specs=[head, whole, whole],
        out_shape=[struct(LEN, GROUP * HD), struct(LEN, HD), struct(LEN, HD)],
        scratch_shapes=[
            pltpu.VMEM((HD, LEN), BF),
            pltpu.VMEM((LEN, HD), F32),
            pltpu.VMEM((LEN, HD), F32),
        ],
        compiler_params=params(60),
        cost_estimate=cost(12 * 10**9, 4 * 2**20),
        name="attention_grads",
    )(where_at, queries, keys, values, out_grad, *rope_wide(), before)


def deal_kernel(x_ref, out_ref):
    part = out_ref.shape[2] // (REP * YLO)
    for zz in range(Z):
        for i in range(REP * YLO):
            at = (i * Z + zz) * part
            out_ref[zz, :, i * part : (i + 1) * part] = x_ref[:, at : at + part]


def split_kernel(at_ref, own_ref, other_ref, *out_refs):
    ten = at_ref[2]
    rows = out_refs[0].shape[0] // REP
    for k, out_ref in enumerate(out_refs):
        at = pl.multiple_of(lax.bitwise_xor(ten, k) * rows, rows)
        out_ref[:rows, :] = own_ref[pl.ds(at, rows), :]
        out_ref[rows:, :] = other_ref[pl.ds(at, rows), :]


def place_kernel(at_ref, *refs):
    pieces, out_ref = refs[:TEN], refs[-1]
    ten = at_ref[2]
    for k, piece in enumerate(pieces):
        at = pl.multiple_of(lax.bitwise_xor(ten, k) * HD, HD)
        out_ref[:, pl.ds(at, HD)] = piece[...]


def select_kernel(at_ref, key_ref, value_ref, _, __, out_ref):
    @pl.when(at_ref[0] == 0)
    def _():
        out_ref[...] = key_ref[...]

    @pl.when(at_ref[0] != 0)
    def _():
        out_ref[...] = value_ref[...]


def turn_kernel(at_ref, x_ref, _, __, out_ref):
    z = at_ref[1]
    for j in range(Z // 2):
        one, two = x_ref[lax.rem(z + 2 * j, Z)], x_ref[lax.rem(z + 2 * j + 1, Z)]
        pair = jnp.concatenate([one, two])
        out_ref[:, j * pair.shape[0] : (j + 1) * pair.shape[0]] = pair.T


def side_weight(weight_ref, y, n):
    at = slice(n * 256, (n + 1) * 256)
    return jnp.concatenate([weight_ref[y * TEN + t, at, :] for t in range(TEN)], axis=1)


def term_kernel(grads_ref, weight_ref, out_ref):
    per = weight_ref.shape[1] // 256
    for y in range(YLO):
        for n in range(per):
            at = (y * per + n) * 256
            term = dot(grads_ref[...], side_weight(weight_ref, y, n), 1, 1)
            out_ref[:, at : at + 256] = term.astype(BF)


def add_kernel(grads_ref, weight_ref, given_ref, *outs):
    rows = outs[0].shape[0]
    per = weight_ref.shape[1] // 256
    for y in range(YLO):
        for n in range(per):
            at = (y * per + n) * 256
            term = dot(grads_ref[...], side_weight(weight_ref, y, n), 1, 1)
            term = (term + given_ref[:, at : at + 256].astype(F32)).astype(BF)
            for j, out_ref in enumerate(outs):
                out_ref[:, at : at + 256] = term[j * rows : (j + 1) * rows, :]


def weight_grad_kernel(h_own, h_other, *refs):
    near, (far_up, far_down, out_ref, own_ref, other_ref) = refs[: Z - 1], refs[Z - 1 :]
    rows = far_up.shape[0]
    for j in range(Z):
        at = slice(j * rows, (j + 1) * rows)
        if j == Z // 2:
            own_ref[at, :] = far_up[...]
            other_ref[at, :] = far_down[...]
        else:
            piece = near[j - (j > Z // 2)]
            own_ref[at, :] = piece[:rows, :]
            other_ref[at, :] = piece[rows:, :]
    out_rows = out_ref.shape[3]
    for pair in range(TEN // 2):
        cols = slice(pair * 2 * HD, (pair + 1) * 2 * HD)
        for r in range(REP):
            for y in range(YLO):
                at = slice((r * YLO + y) * out_rows, (r * YLO + y + 1) * out_rows)
                part = dot(h_own[at, :], own_ref[:, cols], 1, 0)
                part = (part + dot(h_other[at, :], other_ref[:, cols], 1, 0)).astype(BF)
                out_ref[y, 2 * pair, r] = part[:, :HD]
                out_ref[y, 2 * pair + 1, r] = part[:, HD:]


def sum_kernel(at_ref, x_ref, *refs):
    kept_ref, given_ref = refs[-2:]
    rep = at_ref[0]
    for core, out_ref in ((rep, kept_ref), (1 - rep, given_ref)):
        total = x_ref[0, core].astype(F32)
        for i in range(1, x_ref.shape[0]):
            total = total + x_ref[i, core].astype(F32)
        out_ref[...] = total


def join_kernel(at_ref, *refs):
    *pieces, out_ref = refs
    z = at_ref[1]
    part = pieces[0].shape[1] // YLO
    for s, piece in enumerate(pieces):
        source = lax.rem(z - s + Z, Z)
        for y in range(YLO):
            at = pl.multiple_of((y * Z + source) * part, part)
            out_ref[:, pl.ds(at, part)] = piece[:, y * part : (y + 1) * part]


def ring(both):
    rows = both.shape[0] // 2
    up, down = [both], [both]
    for _ in range(Z // 2 - 1):
        up.append(shift(up[-1], "z", Z, 1))
        down.append(shift(down[-1], "z", Z, -1))
    far_up = shift(up[-1][:rows], "z", Z, 1)
    far_down = shift(down[-1][rows:], "z", Z, -1)
    return down + up[:0:-1], far_up, far_down


def on_device(hidden_in, queries, keys, values, out_grad, w_key, w_value, adam_state):
    rep, z, ten = (lax.axis_index(name) for name in ("rep", "z", "tensor"))
    where_at = jnp.stack([rep, z, ten]).astype(jnp.int32)
    first = rep == 0
    state_backup = shift(adam_state, "rep", REP, 1)
    rows, width = hidden_in.shape
    out_rows = width // (REP * YLO * Z)
    w_rows = width // (YLO * Z)

    hidden = pl.pallas_call(
        deal_kernel,
        grid=(4,),
        in_specs=[pl.BlockSpec((rows // 4, width), lambda i: (i, 0))],
        out_specs=pl.BlockSpec((Z, rows // 4, REP * YLO * out_rows), lambda i: (0, i, 0)),
        out_shape=struct(Z, rows, REP * YLO * out_rows),
        compiler_params=params(16),
        cost_estimate=cost(0, 2 * 2**20),
        name="deal",
    )(hidden_in)
    hidden = lax.all_to_all(hidden, "z", split_axis=0, concat_axis=0, tiled=True)

    query_grad, own, other = attention_grads(where_at, queries, keys, values, out_grad, state_backup)
    other = shift(other, "rep", REP, 1)
    pieces = pl.pallas_call(
        split_kernel,
        in_specs=[SMEM, VMEM, VMEM],
        out_specs=[VMEM] * TEN,
        out_shape=[struct(REP * rows, HD)] * TEN,
        compiler_params=params(8),
        cost_estimate=cost(0, 2**19),
        name="split",
    )(where_at, own, other)
    moved = {0: pieces[0]}
    for k in (5, 4, 7, 6, 1, 3, 2):
        moved[k] = lax.ppermute(pieces[k], "tensor", [(i, i ^ k) for i in range(TEN)])
    grads = pl.pallas_call(
        place_kernel,
        in_specs=[SMEM] + [VMEM] * TEN + [ANY],
        out_specs=VMEM,
        out_shape=struct(REP * rows, TEN * HD),
        compiler_params=params(8),
        cost_estimate=cost(0, 2**19),
        name="place",
    )(where_at, *[moved[k] for k in range(TEN)], hidden)

    near, far_up, far_down = ring(grads)

    weight = pl.pallas_call(
        select_kernel,
        in_specs=[SMEM, VMEM, VMEM, ANY, ANY],
        out_specs=VMEM,
        out_shape=struct(w_rows, HD),
        compiler_params=params(8),
        cost_estimate=cost(0, 2**18),
        name="select",
    )(where_at, w_key, w_value, near[1], near[-1])
    weight = jnp.broadcast_to(weight[None], (YLO * TEN,) + weight.shape)
    weight = lax.all_to_all(weight, PLANE, split_axis=0, concat_axis=0, tiled=True)

    hidden = pl.pallas_call(
        turn_kernel,
        in_specs=[SMEM, VMEM, ANY, ANY],
        out_specs=VMEM,
        out_shape=struct(REP * YLO * out_rows, Z * rows),
        compiler_params=params(16),
        cost_estimate=cost(0, 2 * 2**20),
        name="turn",
    )(where_at, hidden, near[2], near[-2])
    hidden_other = shift(hidden, "rep", REP, 1)

    half = struct(Z * rows, TEN * HD)
    partial, grads_own, grads_other = pl.pallas_call(
        weight_grad_kernel,
        in_specs=[VMEM] * (Z + 3),
        out_specs=[VMEM] * 3,
        out_shape=[struct(YLO, TEN, REP, out_rows, HD), half, half],
        compiler_params=params(48),
        cost_estimate=cost(2 * 2**30, 8 * 2**20),
        name="weight_grad",
    )(hidden, hidden_other, *near, far_up, far_down)
    given = pl.pallas_call(
        term_kernel,
        in_specs=[VMEM] * 2,
        out_specs=VMEM,
        out_shape=struct(Z * rows, YLO * w_rows),
        compiler_params=params(24),
        cost_estimate=cost(2**30, 4 * 2**20),
        name="term",
    )(grads_other, weight)
    given = shift(given, "rep", REP, 1)
    partial = partial.reshape(YLO * TEN, REP, out_rows, HD)
    partial = lax.all_to_all(partial, PLANE, split_axis=0, concat_axis=0, tiled=True)

    pieces = pl.pallas_call(
        add_kernel,
        in_specs=[VMEM] * 3,
        out_specs=[VMEM] * Z,
        out_shape=[struct(rows, YLO * w_rows)] * Z,
        compiler_params=params(24),
        cost_estimate=cost(2**30, 5 * 2**20),
        name="add",
    )(grads_own, weight, given)
    moved = {0: pieces[0]}
    for k in (4, 3, 5, 2, 6, 1, 7):
        moved[k] = shift(pieces[k], "z", Z, k)
    moved = [moved[k] for k in range(Z)]
    input_grad = pl.pallas_call(
        join_kernel,
        in_specs=[SMEM] + [VMEM] * Z,
        out_specs=VMEM,
        out_shape=struct(rows, width),
        compiler_params=params(16),
        cost_estimate=cost(0, 2 * 2**20),
        name="join",
    )(where_at, *moved)

    kept, passed = pl.pallas_call(
        sum_kernel,
        in_specs=[SMEM, VMEM] + [ANY] * (Z - 1),
        out_specs=[VMEM] * 2,
        out_shape=[struct(out_rows, HD, dtype=F32)] * 2,
        compiler_params=params(16),
        cost_estimate=cost(0, 2 * 2**20),
        name="sum",
    )(where_at, partial, *moved[1:])
    passed = shift(passed, "rep", REP, 1)
    key_weight_grad = jnp.where(first, kept, passed)
    value_weight_grad = jnp.where(first, passed, kept)
    return (query_grad, input_grad, key_weight_grad, value_weight_grad, state_backup)


def solution(mesh):
    fine = Mesh(mesh.devices.reshape(REP, YLO, Z, TEN), ("rep", "ylo", "z", "tensor"))
    seqs = ("rep", "ylo", "z")
    return jax.shard_map(
        on_device,
        mesh=fine,
        in_specs=(
            P(seqs + ("tensor",), None),
            P(seqs, "tensor"),
            P(seqs, "tensor"),
            P(seqs, "tensor"),
            P(seqs, "tensor"),
            P(("ylo", "z"), "tensor"),
            P(("ylo", "z"), "tensor"),
            P(None, None, seqs, "tensor"),
        ),
        out_specs=(
            P(seqs, "tensor"),
            P(seqs + ("tensor",), None),
            P(seqs, "tensor"),
            P(seqs, "tensor"),
            P(None, None, seqs, "tensor"),
        ),
        check_vma=False,
    )
```

```python
import math

import jax
import jax.numpy as jnp
import numpy as np
from jax import lax
from jax.experimental import pallas as pl
from jax.experimental.pallas import tpu as pltpu
from jax.sharding import Mesh
from jax.sharding import PartitionSpec as P

HEADS = 64
KVH = 8
HD = 128
GROUP = HEADS // KVH
LEN = 512
REP, YLO, Z, TEN = 2, 2, 8, 8
PLANE = ("ylo", "tensor")
SCALE = 1.0 / math.sqrt(HD)
QB = 256
STEP_HEADS = 2
BF, F32 = jnp.bfloat16, jnp.float32

VMEM = pl.BlockSpec(memory_space=pltpu.VMEM)
SMEM = pl.BlockSpec(memory_space=pltpu.SMEM)
ANY = pl.BlockSpec(memory_space=pl.ANY)
HBM = pl.BlockSpec(memory_space=pltpu.HBM)


def dot(a, b, ca, cb):
    return lax.dot_general(a, b, (((ca,), (cb,)), ((), ())), preferred_element_type=F32)


def struct(*shape, dtype=BF):
    return jax.ShapeDtypeStruct(shape, dtype)


def params(mib):
    return pltpu.CompilerParams(vmem_limit_bytes=mib * 2**20)


def cost(flops, nbytes):
    return pl.CostEstimate(flops=flops, bytes_accessed=nbytes, transcendentals=0)


def shift(block, axis, count, by):
    return lax.ppermute(block, axis, [(i, (i + by) % count) for i in range(count)])


def rope_wide():
    half = HD // 2
    angle = np.arange(LEN)[:, None] * 1000000.0 ** (-2.0 * np.arange(half) / HD)[None, :]
    cosine, sine = np.cos(angle), np.sin(angle)
    wide = np.concatenate([cosine, cosine], 1), np.concatenate([sine, -sine], 1)
    return [jnp.asarray(t.astype(np.float32)) for t in wide]


def attention_kernel(at_ref, q_ref, k_ref, v_ref, g_ref, c_ref, s_ref, qg_ref, own_ref, other_ref, kt, dk, dv):
    step = pl.program_id(0)

    @pl.when(step == 0)
    def _():
        kt[...] = k_ref[...].T
        dk[...] = jnp.zeros_like(dk)
        dv[...] = jnp.zeros_like(dv)

    key_at = lax.broadcasted_iota(jnp.int32, (QB, QB), 0)
    query_at = lax.broadcasted_iota(jnp.int32, (QB, QB), 1)
    allowed = key_at <= query_at
    for h in range(STEP_HEADS):
        lanes = slice(h * HD, (h + 1) * HD)
        for block in range(LEN // QB):
            rows = slice(block * QB, (block + 1) * QB)
            span = (block + 1) * QB
            q, g = q_ref[rows, lanes], g_ref[rows, lanes]
            scores = dot(k_ref[:span, :], q, 1, 1)
            scores = [scores[i * QB : (i + 1) * QB] for i in range(block + 1)]
            scores[-1] = jnp.where(allowed, scores[-1], -jnp.inf)
            scores = jnp.concatenate(scores, axis=0)
            top = jnp.max(scores, axis=0, keepdims=True)
            weights = jnp.exp2((scores - top) * (SCALE * math.log2(math.e)))
            inverse = 1.0 / jnp.sum(weights, axis=0, keepdims=True)
            probs = weights * inverse
            dprobs = dot(v_ref[:span, :], g, 1, 1)
            delta = jnp.sum(probs * dprobs, axis=0, keepdims=True)
            dscores = (probs * ((dprobs - delta) * SCALE)).astype(BF)
            dk[:span, :] += dot(dscores, q, 1, 0)
            dv[:span, :] += dot(probs.astype(BF), g, 1, 0)
            qg_ref[rows, lanes] = dot(kt[:, :span], dscores, 1, 0).T.astype(BF)

    @pl.when(step == GROUP // STEP_HEADS - 1)
    def _():
        rotated = dk[...]
        turned = pltpu.roll(rotated, HD // 2, 1)
        key_grad = (rotated * c_ref[...] + turned * s_ref[...]).astype(BF)
        value_grad = dv[...].astype(BF)

        @pl.when(at_ref[0] == 0)
        def _():
            own_ref[...] = key_grad
            other_ref[...] = value_grad

        @pl.when(at_ref[0] != 0)
        def _():
            own_ref[...] = value_grad
            other_ref[...] = key_grad


def attention_grads(where_at, queries, keys, values, out_grad):
    whole = pl.BlockSpec((LEN, HD), lambda h: (0, 0))
    head = pl.BlockSpec((LEN, STEP_HEADS * HD), lambda h: (0, h))
    return pl.pallas_call(
        attention_kernel,
        grid=(GROUP // STEP_HEADS,),
        in_specs=[SMEM, head, whole, whole, head, whole, whole],
        out_specs=[head, whole, whole],
        out_shape=[struct(LEN, GROUP * HD), struct(LEN, HD), struct(LEN, HD)],
        scratch_shapes=[
            pltpu.VMEM((HD, LEN), BF),
            pltpu.VMEM((LEN, HD), F32),
            pltpu.VMEM((LEN, HD), F32),
        ],
        compiler_params=params(60),
        cost_estimate=cost(12 * 10**9, 4 * 2**20),
        name="attention_grads",
    )(where_at, queries, keys, values, out_grad, *rope_wide())


def deal_kernel(x_ref, out_ref):
    part = out_ref.shape[2] // (REP * YLO)
    for zz in range(Z):
        for i in range(REP * YLO):
            at = (i * Z + zz) * part
            out_ref[zz, :, i * part : (i + 1) * part] = x_ref[:, at : at + part]


def split_kernel(at_ref, own_ref, other_ref, *out_refs):
    ten = at_ref[2]
    rows = out_refs[0].shape[0] // REP
    for k, out_ref in enumerate(out_refs):
        at = pl.multiple_of(lax.bitwise_xor(ten, k) * rows, rows)
        out_ref[:rows, :] = own_ref[pl.ds(at, rows), :]
        out_ref[rows:, :] = other_ref[pl.ds(at, rows), :]


def place_kernel(at_ref, *refs):
    pieces, out_ref = refs[:TEN], refs[-1]
    ten = at_ref[2]
    for k, piece in enumerate(pieces):
        at = pl.multiple_of(lax.bitwise_xor(ten, k) * HD, HD)
        out_ref[:, pl.ds(at, HD)] = piece[...]


def select_kernel(at_ref, key_ref, value_ref, _, out_ref):
    @pl.when(at_ref[0] == 0)
    def _():
        out_ref[...] = key_ref[...]

    @pl.when(at_ref[0] != 0)
    def _():
        out_ref[...] = value_ref[...]


def turn_kernel(at_ref, x_ref, _, __, out_ref):
    z = at_ref[1]
    for j in range(Z // 2):
        one, two = x_ref[lax.rem(z + 2 * j, Z)], x_ref[lax.rem(z + 2 * j + 1, Z)]
        pair = jnp.concatenate([one, two])
        out_ref[:, j * pair.shape[0] : (j + 1) * pair.shape[0]] = pair.T


def side_weight(weight_ref, y, n):
    at = slice(n * 256, (n + 1) * 256)
    return jnp.concatenate([weight_ref[y * TEN + t, at, :] for t in range(TEN)], axis=1)


def term_kernel(grads_ref, weight_ref, out_ref):
    per = weight_ref.shape[1] // 256
    for y in range(YLO):
        for n in range(per):
            at = (y * per + n) * 256
            term = dot(grads_ref[...], side_weight(weight_ref, y, n), 1, 1)
            out_ref[:, at : at + 256] = term.astype(BF)


def add_kernel(grads_ref, weight_ref, given_ref, *outs):
    rows = outs[0].shape[0]
    per = weight_ref.shape[1] // 256
    for y in range(YLO):
        for n in range(per):
            at = (y * per + n) * 256
            term = dot(grads_ref[...], side_weight(weight_ref, y, n), 1, 1)
            term = (term + given_ref[:, at : at + 256].astype(F32)).astype(BF)
            for j, out_ref in enumerate(outs):
                out_ref[:, at : at + 256] = term[j * rows : (j + 1) * rows, :]


def weight_grad_kernel(h_own, h_other, *refs):
    near, (far_up, far_down, state_ref) = refs[: Z - 1], refs[Z - 1 : Z + 2]
    out_ref, own_ref, other_ref, state_out, sem = refs[Z + 2 :]
    rows = far_up.shape[0]
    passing = pltpu.make_async_copy(state_ref, state_out, sem)
    passing.start()
    for j in range(Z):
        at = slice(j * rows, (j + 1) * rows)
        if j == Z // 2:
            own_ref[at, :] = far_up[...]
            other_ref[at, :] = far_down[...]
        else:
            piece = near[j - (j > Z // 2)]
            own_ref[at, :] = piece[:rows, :]
            other_ref[at, :] = piece[rows:, :]
    out_rows = out_ref.shape[3]
    for pair in range(TEN // 2):
        cols = slice(pair * 2 * HD, (pair + 1) * 2 * HD)
        for r in range(REP):
            for y in range(YLO):
                at = slice((r * YLO + y) * out_rows, (r * YLO + y + 1) * out_rows)
                part = dot(h_own[at, :], own_ref[:, cols], 1, 0)
                part = (part + dot(h_other[at, :], other_ref[:, cols], 1, 0)).astype(BF)
                out_ref[y, 2 * pair, r] = part[:, :HD]
                out_ref[y, 2 * pair + 1, r] = part[:, HD:]
    passing.wait()


def sum_kernel(at_ref, x_ref, *refs):
    kept_ref, given_ref = refs[-2:]
    rep = at_ref[0]
    for core, out_ref in ((rep, kept_ref), (1 - rep, given_ref)):
        total = x_ref[0, core].astype(F32)
        for i in range(1, x_ref.shape[0]):
            total = total + x_ref[i, core].astype(F32)
        out_ref[...] = total


def join_kernel(at_ref, *refs):
    *pieces, out_ref = refs
    z = at_ref[1]
    part = pieces[0].shape[1] // YLO
    for s, piece in enumerate(pieces):
        source = lax.rem(z - s + Z, Z)
        for y in range(YLO):
            at = pl.multiple_of((y * Z + source) * part, part)
            out_ref[:, pl.ds(at, part)] = piece[:, y * part : (y + 1) * part]


def ring(both):
    rows = both.shape[0] // 2
    up, down = [both], [both]
    for _ in range(Z // 2 - 1):
        up.append(shift(up[-1], "z", Z, 1))
        down.append(shift(down[-1], "z", Z, -1))
    far_up = shift(up[-1][:rows], "z", Z, 1)
    far_down = shift(down[-1][rows:], "z", Z, -1)
    return down + up[:0:-1], far_up, far_down


def on_device(hidden_in, queries, keys, values, out_grad, w_key, w_value, adam_state):
    rep, z, ten = (lax.axis_index(name) for name in ("rep", "z", "tensor"))
    where_at = jnp.stack([rep, z, ten]).astype(jnp.int32)
    first = rep == 0
    state_backup = shift(adam_state, "rep", REP, 1)
    rows, width = hidden_in.shape
    out_rows = width // (REP * YLO * Z)
    w_rows = width // (YLO * Z)

    hidden = pl.pallas_call(
        deal_kernel,
        grid=(4,),
        in_specs=[pl.BlockSpec((rows // 4, width), lambda i: (i, 0))],
        out_specs=pl.BlockSpec((Z, rows // 4, REP * YLO * out_rows), lambda i: (0, i, 0)),
        out_shape=struct(Z, rows, REP * YLO * out_rows),
        compiler_params=params(16),
        cost_estimate=cost(0, 2 * 2**20),
        name="deal",
    )(hidden_in)
    hidden = lax.all_to_all(hidden, "z", split_axis=0, concat_axis=0, tiled=True)

    query_grad, own, other = attention_grads(where_at, queries, keys, values, out_grad)
    other = shift(other, "rep", REP, 1)
    pieces = pl.pallas_call(
        split_kernel,
        in_specs=[SMEM, VMEM, VMEM],
        out_specs=[VMEM] * TEN,
        out_shape=[struct(REP * rows, HD)] * TEN,
        compiler_params=params(8),
        cost_estimate=cost(0, 2**19),
        name="split",
    )(where_at, own, other)
    moved = {0: pieces[0]}
    for k in (5, 4, 7, 6, 1, 3, 2):
        moved[k] = lax.ppermute(pieces[k], "tensor", [(i, i ^ k) for i in range(TEN)])
    grads = pl.pallas_call(
        place_kernel,
        in_specs=[SMEM] + [VMEM] * TEN + [ANY],
        out_specs=VMEM,
        out_shape=struct(REP * rows, TEN * HD),
        compiler_params=params(8),
        cost_estimate=cost(0, 2**19),
        name="place",
    )(where_at, *[moved[k] for k in range(TEN)], hidden)

    near, far_up, far_down = ring(grads)

    weight = pl.pallas_call(
        select_kernel,
        in_specs=[SMEM, VMEM, VMEM, ANY],
        out_specs=VMEM,
        out_shape=struct(w_rows, HD),
        compiler_params=params(8),
        cost_estimate=cost(0, 2**18),
        name="select",
    )(where_at, w_key, w_value, grads)
    weight = jnp.broadcast_to(weight[None], (YLO * TEN,) + weight.shape)
    weight = lax.all_to_all(weight, PLANE, split_axis=0, concat_axis=0, tiled=True)

    hidden = pl.pallas_call(
        turn_kernel,
        in_specs=[SMEM, VMEM, ANY, ANY],
        out_specs=VMEM,
        out_shape=struct(REP * YLO * out_rows, Z * rows),
        compiler_params=params(16),
        cost_estimate=cost(0, 2 * 2**20),
        name="turn",
    )(where_at, hidden, near[2], near[-2])
    hidden_other = shift(hidden, "rep", REP, 1)

    half = struct(Z * rows, TEN * HD)
    state = jax.ShapeDtypeStruct(adam_state.shape, adam_state.dtype)
    partial, grads_own, grads_other, state_backup = pl.pallas_call(
        weight_grad_kernel,
        in_specs=[VMEM] * (Z + 3) + [ANY],
        out_specs=[VMEM] * 3 + [HBM],
        out_shape=[struct(YLO, TEN, REP, out_rows, HD), half, half, state],
        scratch_shapes=[pltpu.SemaphoreType.DMA],
        compiler_params=params(48),
        cost_estimate=cost(2 * 2**31, 8 * 2**20),
        name="weight_grad",
    )(hidden, hidden_other, *near, far_up, far_down, state_backup)
    given = pl.pallas_call(
        term_kernel,
        in_specs=[VMEM] * 2,
        out_specs=VMEM,
        out_shape=struct(Z * rows, YLO * w_rows),
        compiler_params=params(24),
        cost_estimate=cost(2**30, 4 * 2**20),
        name="term",
    )(grads_other, weight)
    given = shift(given, "rep", REP, 1)
    partial = partial.reshape(YLO * TEN, REP, out_rows, HD)
    partial = lax.all_to_all(partial, PLANE, split_axis=0, concat_axis=0, tiled=True)

    pieces = pl.pallas_call(
        add_kernel,
        in_specs=[VMEM] * 3,
        out_specs=[VMEM] * Z,
        out_shape=[struct(rows, YLO * w_rows)] * Z,
        compiler_params=params(24),
        cost_estimate=cost(2**30, 5 * 2**20),
        name="add",
    )(grads_own, weight, given)
    moved = {0: pieces[0]}
    for k in (4, 3, 5, 2, 6, 1, 7):
        moved[k] = shift(pieces[k], "z", Z, k)
    moved = [moved[k] for k in range(Z)]
    input_grad = pl.pallas_call(
        join_kernel,
        in_specs=[SMEM] + [VMEM] * Z,
        out_specs=VMEM,
        out_shape=struct(rows, width),
        compiler_params=params(16),
        cost_estimate=cost(0, 2 * 2**20),
        name="join",
    )(where_at, *moved)

    kept, passed = pl.pallas_call(
        sum_kernel,
        in_specs=[SMEM, VMEM] + [ANY] * 3,
        out_specs=[VMEM] * 2,
        out_shape=[struct(out_rows, HD, dtype=F32)] * 2,
        compiler_params=params(16),
        cost_estimate=cost(0, 2 * 2**20),
        name="sum",
    )(where_at, partial, moved[4], moved[3], moved[5])
    passed = shift(passed, "rep", REP, 1)
    key_weight_grad = jnp.where(first, kept, passed)
    value_weight_grad = jnp.where(first, passed, kept)
    return (query_grad, input_grad, key_weight_grad, value_weight_grad, state_backup)


def solution(mesh):
    fine = Mesh(mesh.devices.reshape(REP, YLO, Z, TEN), ("rep", "ylo", "z", "tensor"))
    seqs = ("rep", "ylo", "z")
    return jax.shard_map(
        on_device,
        mesh=fine,
        in_specs=(
            P(seqs + ("tensor",), None),
            P(seqs, "tensor"),
            P(seqs, "tensor"),
            P(seqs, "tensor"),
            P(seqs, "tensor"),
            P(("ylo", "z"), "tensor"),
            P(("ylo", "z"), "tensor"),
            P(None, None, seqs, "tensor"),
        ),
        out_specs=(
            P(seqs, "tensor"),
            P(seqs + ("tensor",), None),
            P(seqs, "tensor"),
            P(seqs, "tensor"),
            P(None, None, seqs, "tensor"),
        ),
        check_vma=False,
    )
```

```python
import math

import jax
import jax.numpy as jnp
import numpy as np
from jax import lax
from jax.experimental import pallas as pl
from jax.experimental.pallas import tpu as pltpu
from jax.sharding import Mesh
from jax.sharding import PartitionSpec as P

HEADS = 64
KVH = 8
HD = 128
GROUP = HEADS // KVH
LEN = 512
REP, YLO, Z, TEN = 2, 2, 8, 8
PLANE = ("ylo", "tensor")
SCALE = 1.0 / math.sqrt(HD)
QB = 256
STEP_HEADS = 4
BF, F32 = jnp.bfloat16, jnp.float32

VMEM = pl.BlockSpec(memory_space=pltpu.VMEM)
SMEM = pl.BlockSpec(memory_space=pltpu.SMEM)
ANY = pl.BlockSpec(memory_space=pl.ANY)
HBM = pl.BlockSpec(memory_space=pltpu.HBM)


def dot(a, b, ca, cb):
    return lax.dot_general(a, b, (((ca,), (cb,)), ((), ())), preferred_element_type=F32)


def struct(*shape, dtype=BF):
    return jax.ShapeDtypeStruct(shape, dtype)


def params(mib):
    return pltpu.CompilerParams(vmem_limit_bytes=mib * 2**20)


def cost(flops, nbytes):
    return pl.CostEstimate(flops=flops, bytes_accessed=nbytes, transcendentals=0)


def shift(block, axis, count, by):
    return lax.ppermute(block, axis, [(i, (i + by) % count) for i in range(count)])


def rope_wide():
    half = HD // 2
    angle = np.arange(LEN)[:, None] * 1000000.0 ** (-2.0 * np.arange(half) / HD)[None, :]
    cosine, sine = np.cos(angle), np.sin(angle)
    wide = np.concatenate([cosine, cosine], 1), np.concatenate([sine, -sine], 1)
    return [jnp.asarray(t.astype(np.float32)) for t in wide]


def attention_kernel(at_ref, q_ref, k_ref, v_ref, g_ref, c_ref, s_ref, qg_ref, own_ref, other_ref, kt, dk, dv):
    step = pl.program_id(0)

    @pl.when(step == 0)
    def _():
        kt[...] = k_ref[...].T
        dk[...] = jnp.zeros_like(dk)
        dv[...] = jnp.zeros_like(dv)

    key_at = lax.broadcasted_iota(jnp.int32, (QB, QB), 0)
    query_at = lax.broadcasted_iota(jnp.int32, (QB, QB), 1)
    allowed = key_at <= query_at
    for h in range(STEP_HEADS):
        lanes = slice(h * HD, (h + 1) * HD)
        for block in range(LEN // QB):
            rows = slice(block * QB, (block + 1) * QB)
            span = (block + 1) * QB
            q, g = q_ref[rows, lanes], g_ref[rows, lanes]
            scores = dot(k_ref[:span, :], q, 1, 1)
            scores = [scores[i * QB : (i + 1) * QB] for i in range(block + 1)]
            scores[-1] = jnp.where(allowed, scores[-1], -jnp.inf)
            scores = jnp.concatenate(scores, axis=0)
            top = jnp.max(scores, axis=0, keepdims=True)
            weights = jnp.exp2((scores - top) * (SCALE * math.log2(math.e)))
            inverse = 1.0 / jnp.sum(weights, axis=0, keepdims=True)
            probs = weights * inverse
            dprobs = dot(v_ref[:span, :], g, 1, 1)
            delta = jnp.sum(probs * dprobs, axis=0, keepdims=True)
            dscores = (probs * ((dprobs - delta) * SCALE)).astype(BF)
            dk[:span, :] += dot(dscores, q, 1, 0)
            dv[:span, :] += dot(probs.astype(BF), g, 1, 0)
            qg_ref[rows, lanes] = dot(kt[:, :span], dscores, 1, 0).T.astype(BF)

    @pl.when(step == GROUP // STEP_HEADS - 1)
    def _():
        rotated = dk[...]
        turned = pltpu.roll(rotated, HD // 2, 1)
        key_grad = (rotated * c_ref[...] + turned * s_ref[...]).astype(BF)
        value_grad = dv[...].astype(BF)

        @pl.when(at_ref[0] == 0)
        def _():
            own_ref[...] = key_grad
            other_ref[...] = value_grad

        @pl.when(at_ref[0] != 0)
        def _():
            own_ref[...] = value_grad
            other_ref[...] = key_grad


def attention_grads(where_at, queries, keys, values, out_grad):
    whole = pl.BlockSpec((LEN, HD), lambda h: (0, 0))
    head = pl.BlockSpec((LEN, STEP_HEADS * HD), lambda h: (0, h))
    return pl.pallas_call(
        attention_kernel,
        grid=(GROUP // STEP_HEADS,),
        in_specs=[SMEM, head, whole, whole, head, whole, whole],
        out_specs=[head, whole, whole],
        out_shape=[struct(LEN, GROUP * HD), struct(LEN, HD), struct(LEN, HD)],
        scratch_shapes=[
            pltpu.VMEM((HD, LEN), BF),
            pltpu.VMEM((LEN, HD), F32),
            pltpu.VMEM((LEN, HD), F32),
        ],
        compiler_params=params(60),
        cost_estimate=cost(12 * 10**9, 4 * 2**20),
        name="attention_grads",
    )(where_at, queries, keys, values, out_grad, *rope_wide())


def deal_kernel(x_ref, out_ref):
    part = out_ref.shape[2] // (REP * YLO)
    for zz in range(Z):
        for i in range(REP * YLO):
            at = (i * Z + zz) * part
            out_ref[zz, :, i * part : (i + 1) * part] = x_ref[:, at : at + part]


def split_kernel(at_ref, own_ref, other_ref, *out_refs):
    ten = at_ref[2]
    rows = out_refs[0].shape[0] // 4
    for k, out_ref in enumerate(out_refs):
        for side in range(2):
            at = pl.multiple_of(lax.bitwise_xor(ten, 2 * k + side) * rows, rows)
            row = 2 * side * rows
            out_ref[row : row + rows, :] = own_ref[pl.ds(at, rows), :]
            out_ref[row + rows : row + 2 * rows, :] = other_ref[pl.ds(at, rows), :]


def middle_kernel(*refs):
    pieces, out_ref = refs[:-1], refs[-1]
    rows = out_ref.shape[1]
    for k, piece in enumerate(pieces):
        out_ref[k] = piece[rows:, :]


def place_kernel(at_ref, *refs):
    pieces, passed_ref, out_ref = refs[: TEN // 2], refs[TEN // 2], refs[-1]
    ten = at_ref[2]
    rows = out_ref.shape[0]
    for k, piece in enumerate(pieces):
        at = pl.multiple_of(lax.bitwise_xor(ten, 2 * k) * HD, HD)
        out_ref[:, pl.ds(at, HD)] = piece[:rows, :]
        at = pl.multiple_of(lax.bitwise_xor(ten, 2 * k + 1) * HD, HD)
        out_ref[:, pl.ds(at, HD)] = passed_ref[k]


def select_kernel(at_ref, key_ref, value_ref, _, out_ref):
    @pl.when(at_ref[0] == 0)
    def _():
        out_ref[...] = key_ref[...]

    @pl.when(at_ref[0] != 0)
    def _():
        out_ref[...] = value_ref[...]


def turn_kernel(at_ref, x_ref, _, __, out_ref):
    z = at_ref[1]
    for j in range(Z // 2):
        one, two = x_ref[lax.rem(z + 2 * j, Z)], x_ref[lax.rem(z + 2 * j + 1, Z)]
        pair = jnp.concatenate([one, two])
        out_ref[:, j * pair.shape[0] : (j + 1) * pair.shape[0]] = pair.T


def side_weight(weight_ref, y, n):
    at = slice(n * 256, (n + 1) * 256)
    return jnp.concatenate([weight_ref[y * TEN + t, at, :] for t in range(TEN)], axis=1)


def term_kernel(grads_ref, weight_ref, out_ref):
    per = weight_ref.shape[1] // 256
    for y in range(YLO):
        for n in range(per):
            at = (y * per + n) * 256
            term = dot(grads_ref[...], side_weight(weight_ref, y, n), 1, 1)
            out_ref[:, at : at + 256] = term.astype(BF)


def add_kernel(grads_ref, weight_ref, given_ref, *outs):
    rows = outs[0].shape[0]
    per = weight_ref.shape[1] // 256
    for y in range(YLO):
        for n in range(per):
            at = (y * per + n) * 256
            term = dot(grads_ref[...], side_weight(weight_ref, y, n), 1, 1)
            term = (term + given_ref[:, at : at + 256].astype(F32)).astype(BF)
            for j, out_ref in enumerate(outs):
                out_ref[:, at : at + 256] = term[j * rows : (j + 1) * rows, :]


def weight_grad_kernel(h_own, h_other, *refs):
    near, (far_up, far_down, state_ref) = refs[: Z - 1], refs[Z - 1 : Z + 2]
    out_ref, own_ref, other_ref, state_out, sem = refs[Z + 2 :]
    rows = far_up.shape[0]
    passing = pltpu.make_async_copy(state_ref, state_out, sem)
    passing.start()
    for j in range(Z):
        at = slice(j * rows, (j + 1) * rows)
        if j == Z // 2:
            own_ref[at, :] = far_up[...]
            other_ref[at, :] = far_down[...]
        else:
            piece = near[j - (j > Z // 2)]
            own_ref[at, :] = piece[:rows, :]
            other_ref[at, :] = piece[rows:, :]
    out_rows = out_ref.shape[3]
    for pair in range(TEN // 2):
        cols = slice(pair * 2 * HD, (pair + 1) * 2 * HD)
        for r in range(REP):
            for y in range(YLO):
                at = slice((r * YLO + y) * out_rows, (r * YLO + y + 1) * out_rows)
                part = dot(h_own[at, :], own_ref[:, cols], 1, 0)
                part = (part + dot(h_other[at, :], other_ref[:, cols], 1, 0)).astype(BF)
                out_ref[y, 2 * pair, r] = part[:, :HD]
                out_ref[y, 2 * pair + 1, r] = part[:, HD:]
    passing.wait()


def sum_kernel(at_ref, x_ref, *refs):
    kept_ref, given_ref = refs[-2:]
    rep = at_ref[0]
    for core, out_ref in ((rep, kept_ref), (1 - rep, given_ref)):
        total = x_ref[0, core].astype(F32)
        for i in range(1, x_ref.shape[0]):
            total = total + x_ref[i, core].astype(F32)
        out_ref[...] = total


def join_kernel(at_ref, *refs):
    *pieces, out_ref = refs
    z = at_ref[1]
    part = pieces[0].shape[1] // YLO
    for s, piece in enumerate(pieces):
        source = lax.rem(z - s + Z, Z)
        for y in range(YLO):
            at = pl.multiple_of((y * Z + source) * part, part)
            out_ref[:, pl.ds(at, part)] = piece[:, y * part : (y + 1) * part]


def ring(both):
    rows = both.shape[0] // 2
    up, down = [both], [both]
    for _ in range(Z // 2 - 1):
        up.append(shift(up[-1], "z", Z, 1))
        down.append(shift(down[-1], "z", Z, -1))
    far_up = shift(up[-1][:rows], "z", Z, 1)
    far_down = shift(down[-1][rows:], "z", Z, -1)
    return down + up[:0:-1], far_up, far_down


def on_device(hidden_in, queries, keys, values, out_grad, w_key, w_value, adam_state):
    rep, z, ten = (lax.axis_index(name) for name in ("rep", "z", "tensor"))
    where_at = jnp.stack([rep, z, ten]).astype(jnp.int32)
    first = rep == 0
    state_backup = shift(adam_state, "rep", REP, 1)
    rows, width = hidden_in.shape
    out_rows = width // (REP * YLO * Z)
    w_rows = width // (YLO * Z)

    hidden = pl.pallas_call(
        deal_kernel,
        grid=(4,),
        in_specs=[pl.BlockSpec((rows // 4, width), lambda i: (i, 0))],
        out_specs=pl.BlockSpec((Z, rows // 4, REP * YLO * out_rows), lambda i: (0, i, 0)),
        out_shape=struct(Z, rows, REP * YLO * out_rows),
        compiler_params=params(16),
        cost_estimate=cost(0, 2 * 2**20),
        name="deal",
    )(hidden_in)
    hidden = lax.all_to_all(hidden, "z", split_axis=0, concat_axis=0, tiled=True)

    query_grad, own, other = attention_grads(where_at, queries, keys, values, out_grad)
    other = shift(other, "rep", REP, 1)
    pieces = pl.pallas_call(
        split_kernel,
        in_specs=[SMEM, VMEM, VMEM],
        out_specs=[VMEM] * (TEN // 2),
        out_shape=[struct(2 * REP * rows, HD)] * (TEN // 2),
        compiler_params=params(8),
        cost_estimate=cost(0, 2**19),
        name="split",
    )(where_at, own, other)

    def across(block, mask):
        return lax.ppermute(block, "tensor", [(i, i ^ mask) for i in range(TEN)])

    moved = {0: pieces[0]}
    for k in (2, 1, 3):
        moved[k] = across(pieces[k], 2 * k)
    moved = [moved[k] for k in range(TEN // 2)]
    passed = pl.pallas_call(
        middle_kernel,
        in_specs=[VMEM] * (TEN // 2),
        out_specs=VMEM,
        out_shape=struct(TEN // 2, REP * rows, HD),
        compiler_params=params(8),
        cost_estimate=cost(0, 2**18),
        name="middle",
    )(*moved)
    passed = across(passed, 1)
    grads = pl.pallas_call(
        place_kernel,
        in_specs=[SMEM] + [VMEM] * (TEN // 2 + 1) + [ANY],
        out_specs=VMEM,
        out_shape=struct(REP * rows, TEN * HD),
        compiler_params=params(8),
        cost_estimate=cost(0, 2**19),
        name="place",
    )(where_at, *moved, passed, hidden)

    near, far_up, far_down = ring(grads)

    weight = pl.pallas_call(
        select_kernel,
        in_specs=[SMEM, VMEM, VMEM, ANY],
        out_specs=VMEM,
        out_shape=struct(w_rows, HD),
        compiler_params=params(8),
        cost_estimate=cost(0, 2**18),
        name="select",
    )(where_at, w_key, w_value, grads)
    weight = jnp.broadcast_to(weight[None], (YLO * TEN,) + weight.shape)
    weight = lax.all_to_all(weight, PLANE, split_axis=0, concat_axis=0, tiled=True)

    hidden = pl.pallas_call(
        turn_kernel,
        in_specs=[SMEM, VMEM, ANY, ANY],
        out_specs=VMEM,
        out_shape=struct(REP * YLO * out_rows, Z * rows),
        compiler_params=params(16),
        cost_estimate=cost(0, 2 * 2**20),
        name="turn",
    )(where_at, hidden, near[2], near[-2])
    hidden_other = shift(hidden, "rep", REP, 1)

    half = struct(Z * rows, TEN * HD)
    state = jax.ShapeDtypeStruct(adam_state.shape, adam_state.dtype)
    partial, grads_own, grads_other, state_backup = pl.pallas_call(
        weight_grad_kernel,
        in_specs=[VMEM] * (Z + 3) + [ANY],
        out_specs=[VMEM] * 3 + [HBM],
        out_shape=[struct(YLO, TEN, REP, out_rows, HD), half, half, state],
        scratch_shapes=[pltpu.SemaphoreType.DMA],
        compiler_params=params(32),
        cost_estimate=cost(2 * 2**31, 8 * 2**20),
        name="weight_grad",
    )(hidden, hidden_other, *near, far_up, far_down, state_backup)
    given = pl.pallas_call(
        term_kernel,
        in_specs=[VMEM] * 2,
        out_specs=VMEM,
        out_shape=struct(Z * rows, YLO * w_rows),
        compiler_params=params(24),
        cost_estimate=cost(2**30, 4 * 2**20),
        name="term",
    )(grads_other, weight)
    given = shift(given, "rep", REP, 1)
    partial = partial.reshape(YLO * TEN, REP, out_rows, HD)
    partial = lax.all_to_all(partial, PLANE, split_axis=0, concat_axis=0, tiled=True)

    pieces = pl.pallas_call(
        add_kernel,
        in_specs=[VMEM] * 3,
        out_specs=[VMEM] * Z,
        out_shape=[struct(rows, YLO * w_rows)] * Z,
        compiler_params=params(24),
        cost_estimate=cost(2**30, 5 * 2**20),
        name="add",
    )(grads_own, weight, given)
    moved = {0: pieces[0]}
    for k in (4, 3, 5, 2, 6, 1, 7):
        moved[k] = shift(pieces[k], "z", Z, k)
    moved = [moved[k] for k in range(Z)]
    input_grad = pl.pallas_call(
        join_kernel,
        in_specs=[SMEM] + [VMEM] * Z,
        out_specs=VMEM,
        out_shape=struct(rows, width),
        compiler_params=params(16),
        cost_estimate=cost(0, 2 * 2**20),
        name="join",
    )(where_at, *moved)

    kept, passed = pl.pallas_call(
        sum_kernel,
        in_specs=[SMEM, VMEM] + [ANY] * 3,
        out_specs=[VMEM] * 2,
        out_shape=[struct(out_rows, HD, dtype=F32)] * 2,
        compiler_params=params(16),
        cost_estimate=cost(0, 2 * 2**20),
        name="sum",
    )(where_at, partial, moved[4], moved[3], moved[5])
    passed = shift(passed, "rep", REP, 1)
    key_weight_grad = jnp.where(first, kept, passed)
    value_weight_grad = jnp.where(first, passed, kept)
    return (query_grad, input_grad, key_weight_grad, value_weight_grad, state_backup)


def solution(mesh):
    fine = Mesh(mesh.devices.reshape(REP, YLO, Z, TEN), ("rep", "ylo", "z", "tensor"))
    seqs = ("rep", "ylo", "z")
    return jax.shard_map(
        on_device,
        mesh=fine,
        in_specs=(
            P(seqs + ("tensor",), None),
            P(seqs, "tensor"),
            P(seqs, "tensor"),
            P(seqs, "tensor"),
            P(seqs, "tensor"),
            P(("ylo", "z"), "tensor"),
            P(("ylo", "z"), "tensor"),
            P(None, None, seqs, "tensor"),
        ),
        out_specs=(
            P(seqs, "tensor"),
            P(seqs + ("tensor",), None),
            P(seqs, "tensor"),
            P(seqs, "tensor"),
            P(None, None, seqs, "tensor"),
        ),
        check_vma=False,
    )
```

```python
import math

import jax
import jax.numpy as jnp
import numpy as np
from jax import lax
from jax.experimental import pallas as pl
from jax.experimental.pallas import tpu as pltpu
from jax.sharding import Mesh
from jax.sharding import PartitionSpec as P

HEADS = 64
KVH = 8
HD = 128
GROUP = HEADS // KVH
LEN = 512
REP, YLO, Z, TEN = 2, 2, 8, 8
PLANE = ("ylo", "tensor")
SCALE = 1.0 / math.sqrt(HD)
QB = 256
STEP_HEADS = 4
BF, F32 = jnp.bfloat16, jnp.float32

VMEM = pl.BlockSpec(memory_space=pltpu.VMEM)
SMEM = pl.BlockSpec(memory_space=pltpu.SMEM)
ANY = pl.BlockSpec(memory_space=pl.ANY)
HBM = pl.BlockSpec(memory_space=pltpu.HBM)


def dot(a, b, ca, cb):
    return lax.dot_general(a, b, (((ca,), (cb,)), ((), ())), preferred_element_type=F32)


def struct(*shape, dtype=BF):
    return jax.ShapeDtypeStruct(shape, dtype)


def params(mib):
    return pltpu.CompilerParams(vmem_limit_bytes=mib * 2**20)


def cost(flops, nbytes):
    return pl.CostEstimate(flops=flops, bytes_accessed=nbytes, transcendentals=0)


def shift(block, axis, count, by):
    return lax.ppermute(block, axis, [(i, (i + by) % count) for i in range(count)])


def rope_wide():
    half = HD // 2
    angle = np.arange(LEN)[:, None] * 1000000.0 ** (-2.0 * np.arange(half) / HD)[None, :]
    cosine, sine = np.cos(angle), np.sin(angle)
    wide = np.concatenate([cosine, cosine], 1), np.concatenate([sine, -sine], 1)
    return [jnp.asarray(t.astype(np.float32)) for t in wide]


def attention_kernel(q_ref, k_ref, v_ref, g_ref, c_ref, s_ref, qg_ref, own_ref, other_ref, kt, dk, dv):
    step = pl.program_id(0)

    @pl.when(step == 0)
    def _():
        kt[...] = k_ref[...].T
        dk[...] = jnp.zeros_like(dk)
        dv[...] = jnp.zeros_like(dv)

    key_at = lax.broadcasted_iota(jnp.int32, (QB, QB), 0)
    query_at = lax.broadcasted_iota(jnp.int32, (QB, QB), 1)
    allowed = key_at <= query_at
    for h in range(STEP_HEADS):
        lanes = slice(h * HD, (h + 1) * HD)
        for block in range(LEN // QB):
            rows = slice(block * QB, (block + 1) * QB)
            span = (block + 1) * QB
            q, g = q_ref[rows, lanes], g_ref[rows, lanes]
            scores = dot(k_ref[:span, :], q, 1, 1)
            scores = [scores[i * QB : (i + 1) * QB] for i in range(block + 1)]
            scores[-1] = jnp.where(allowed, scores[-1], -jnp.inf)
            scores = jnp.concatenate(scores, axis=0)
            top = jnp.max(scores, axis=0, keepdims=True)
            weights = jnp.exp2((scores - top) * (SCALE * math.log2(math.e)))
            inverse = 1.0 / jnp.sum(weights, axis=0, keepdims=True)
            probs = weights * inverse
            dprobs = dot(v_ref[:span, :], g, 1, 1)
            delta = jnp.sum(probs * dprobs, axis=0, keepdims=True)
            dscores = (probs * ((dprobs - delta) * SCALE)).astype(BF)
            dk[:span, :] += dot(dscores, q, 1, 0)
            dv[:span, :] += dot(probs.astype(BF), g, 1, 0)
            qg_ref[rows, lanes] = dot(kt[:, :span], dscores, 1, 0).T.astype(BF)

    @pl.when(step == GROUP // STEP_HEADS - 1)
    def _():
        rotated = dk[...]
        turned = pltpu.roll(rotated, HD // 2, 1)
        key_grad = (rotated * c_ref[...] + turned * s_ref[...]).astype(BF)
        value_grad = dv[...].astype(BF)

        rep = lax.axis_index("rep")

        @pl.when(rep == 0)
        def _():
            own_ref[...] = key_grad
            other_ref[...] = value_grad

        @pl.when(rep != 0)
        def _():
            own_ref[...] = value_grad
            other_ref[...] = key_grad


def attention_grads(queries, keys, values, out_grad):
    whole = pl.BlockSpec((LEN, HD), lambda h: (0, 0))
    head = pl.BlockSpec((LEN, STEP_HEADS * HD), lambda h: (0, h))
    return pl.pallas_call(
        attention_kernel,
        grid=(GROUP // STEP_HEADS,),
        in_specs=[head, whole, whole, head, whole, whole],
        out_specs=[head, whole, whole],
        out_shape=[struct(LEN, GROUP * HD), struct(LEN, HD), struct(LEN, HD)],
        scratch_shapes=[
            pltpu.VMEM((HD, LEN), BF),
            pltpu.VMEM((LEN, HD), F32),
            pltpu.VMEM((LEN, HD), F32),
        ],
        compiler_params=params(60),
        cost_estimate=cost(12 * 10**9, 4 * 2**20),
        name="attention_grads",
    )(queries, keys, values, out_grad, *rope_wide())


def deal_kernel(x_ref, out_ref):
    part = out_ref.shape[2] // (REP * YLO)
    for zz in range(Z):
        for i in range(REP * YLO):
            at = (i * Z + zz) * part
            out_ref[zz, :, i * part : (i + 1) * part] = x_ref[:, at : at + part]


def split_kernel(at_ref, own_ref, other_ref, *out_refs):
    ten = at_ref[2]
    rows = out_refs[0].shape[0] // 4
    for k, out_ref in enumerate(out_refs):
        for side in range(2):
            at = pl.multiple_of(lax.bitwise_xor(ten, 2 * k + side) * rows, rows)
            row = 2 * side * rows
            out_ref[row : row + rows, :] = own_ref[pl.ds(at, rows), :]
            out_ref[row + rows : row + 2 * rows, :] = other_ref[pl.ds(at, rows), :]


def middle_kernel(*refs):
    pieces, out_ref = refs[:-1], refs[-1]
    rows = out_ref.shape[1]
    for k, piece in enumerate(pieces):
        out_ref[k] = piece[rows:, :]


def place_kernel(at_ref, *refs):
    pieces, passed_ref, out_ref = refs[: TEN // 2], refs[TEN // 2], refs[-1]
    ten = at_ref[2]
    rows = out_ref.shape[0]
    for k, piece in enumerate(pieces):
        at = pl.multiple_of(lax.bitwise_xor(ten, 2 * k) * HD, HD)
        out_ref[:, pl.ds(at, HD)] = piece[:rows, :]
        at = pl.multiple_of(lax.bitwise_xor(ten, 2 * k + 1) * HD, HD)
        out_ref[:, pl.ds(at, HD)] = passed_ref[k]


def select_kernel(at_ref, key_ref, value_ref, _, out_ref):
    @pl.when(at_ref[0] == 0)
    def _():
        out_ref[...] = key_ref[...]

    @pl.when(at_ref[0] != 0)
    def _():
        out_ref[...] = value_ref[...]


def turn_kernel(at_ref, x_ref, _, __, out_ref):
    z = at_ref[1]
    for j in range(Z // 2):
        one, two = x_ref[lax.rem(z + 2 * j, Z)], x_ref[lax.rem(z + 2 * j + 1, Z)]
        pair = jnp.concatenate([one, two])
        out_ref[:, j * pair.shape[0] : (j + 1) * pair.shape[0]] = pair.T


def side_weight(weight_ref, y, n):
    at = slice(n * 256, (n + 1) * 256)
    return jnp.concatenate([weight_ref[y * TEN + t, at, :] for t in range(TEN)], axis=1)


def term_kernel(grads_ref, weight_ref, out_ref):
    per = weight_ref.shape[1] // 256
    for y in range(YLO):
        for n in range(per):
            at = (y * per + n) * 256
            term = dot(grads_ref[...], side_weight(weight_ref, y, n), 1, 1)
            out_ref[:, at : at + 256] = term.astype(BF)


def add_kernel(grads_ref, weight_ref, given_ref, *outs):
    rows = outs[0].shape[0]
    per = weight_ref.shape[1] // 256
    for y in range(YLO):
        for n in range(per):
            at = (y * per + n) * 256
            term = dot(grads_ref[...], side_weight(weight_ref, y, n), 1, 1)
            term = (term + given_ref[:, at : at + 256].astype(F32)).astype(BF)
            for j, out_ref in enumerate(outs):
                out_ref[:, at : at + 256] = term[j * rows : (j + 1) * rows, :]


def weight_grad_kernel(h_own, h_other, *refs):
    near, (far_up, far_down, state_ref) = refs[: Z - 1], refs[Z - 1 : Z + 2]
    out_ref, own_ref, other_ref, state_out, sem = refs[Z + 2 :]
    rows = far_up.shape[0]
    passing = pltpu.make_async_copy(state_ref, state_out, sem)
    passing.start()
    for j in range(Z):
        at = slice(j * rows, (j + 1) * rows)
        if j == Z // 2:
            own_ref[at, :] = far_up[...]
            other_ref[at, :] = far_down[...]
        else:
            piece = near[j - (j > Z // 2)]
            own_ref[at, :] = piece[:rows, :]
            other_ref[at, :] = piece[rows:, :]
    out_rows = out_ref.shape[3]
    for pair in range(TEN // 2):
        cols = slice(pair * 2 * HD, (pair + 1) * 2 * HD)
        for r in range(REP):
            for y in range(YLO):
                at = slice((r * YLO + y) * out_rows, (r * YLO + y + 1) * out_rows)
                part = dot(h_own[at, :], own_ref[:, cols], 1, 0)
                part = (part + dot(h_other[at, :], other_ref[:, cols], 1, 0)).astype(BF)
                out_ref[y, 2 * pair, r] = part[:, :HD]
                out_ref[y, 2 * pair + 1, r] = part[:, HD:]
    passing.wait()


def sum_kernel(at_ref, x_ref, *refs):
    kept_ref, given_ref = refs[-2:]
    rep = at_ref[0]
    for core, out_ref in ((rep, kept_ref), (1 - rep, given_ref)):
        total = x_ref[0, core].astype(F32)
        for i in range(1, x_ref.shape[0]):
            total = total + x_ref[i, core].astype(F32)
        out_ref[...] = total


def join_kernel(at_ref, *refs):
    *pieces, out_ref = refs
    z = at_ref[1]
    part = pieces[0].shape[1] // YLO
    for s, piece in enumerate(pieces):
        source = lax.rem(z - s + Z, Z)
        for y in range(YLO):
            at = pl.multiple_of((y * Z + source) * part, part)
            out_ref[:, pl.ds(at, part)] = piece[:, y * part : (y + 1) * part]


def ring(both):
    rows = both.shape[0] // 2
    up, down = [both], [both]
    for _ in range(Z // 2 - 1):
        up.append(shift(up[-1], "z", Z, 1))
        down.append(shift(down[-1], "z", Z, -1))
    far_up = shift(up[-1][:rows], "z", Z, 1)
    far_down = shift(down[-1][rows:], "z", Z, -1)
    return down + up[:0:-1], far_up, far_down


def on_device(hidden_in, queries, keys, values, out_grad, w_key, w_value, adam_state):
    rep, z, ten = (lax.axis_index(name) for name in ("rep", "z", "tensor"))
    where_at = jnp.stack([rep, z, ten]).astype(jnp.int32)
    first = rep == 0
    state_backup = shift(adam_state, "rep", REP, 1)
    rows, width = hidden_in.shape
    out_rows = width // (REP * YLO * Z)
    w_rows = width // (YLO * Z)

    hidden = pl.pallas_call(
        deal_kernel,
        grid=(2,),
        in_specs=[pl.BlockSpec((rows // 2, width), lambda i: (i, 0))],
        out_specs=pl.BlockSpec((Z, rows // 2, REP * YLO * out_rows), lambda i: (0, i, 0)),
        out_shape=struct(Z, rows, REP * YLO * out_rows),
        compiler_params=params(60),
        cost_estimate=cost(0, 2 * 2**20),
        name="deal",
    )(hidden_in)
    hidden = lax.all_to_all(hidden, "z", split_axis=0, concat_axis=0, tiled=True)

    query_grad, own, other = attention_grads(queries, keys, values, out_grad)
    other = shift(other, "rep", REP, 1)
    pieces = pl.pallas_call(
        split_kernel,
        in_specs=[SMEM, VMEM, VMEM],
        out_specs=[VMEM] * (TEN // 2),
        out_shape=[struct(2 * REP * rows, HD)] * (TEN // 2),
        compiler_params=params(8),
        cost_estimate=cost(0, 2**19),
        name="split",
    )(where_at, own, other)

    def across(block, mask):
        return lax.ppermute(block, "tensor", [(i, i ^ mask) for i in range(TEN)])

    moved = {0: pieces[0]}
    for k in (2, 1, 3):
        moved[k] = across(pieces[k], 2 * k)
    moved = [moved[k] for k in range(TEN // 2)]
    passed = pl.pallas_call(
        middle_kernel,
        in_specs=[VMEM] * (TEN // 2),
        out_specs=VMEM,
        out_shape=struct(TEN // 2, REP * rows, HD),
        compiler_params=params(8),
        cost_estimate=cost(0, 2**18),
        name="middle",
    )(*moved)
    passed = across(passed, 1)
    grads = pl.pallas_call(
        place_kernel,
        in_specs=[SMEM] + [VMEM] * (TEN // 2 + 1) + [ANY],
        out_specs=VMEM,
        out_shape=struct(REP * rows, TEN * HD),
        compiler_params=params(8),
        cost_estimate=cost(0, 2**19),
        name="place",
    )(where_at, *moved, passed, hidden)

    near, far_up, far_down = ring(grads)

    weight = pl.pallas_call(
        select_kernel,
        in_specs=[SMEM, VMEM, VMEM, ANY],
        out_specs=VMEM,
        out_shape=struct(w_rows, HD),
        compiler_params=params(8),
        cost_estimate=cost(0, 2**18),
        name="select",
    )(where_at, w_key, w_value, grads)
    weight = jnp.broadcast_to(weight[None], (YLO * TEN,) + weight.shape)
    weight = lax.all_to_all(weight, PLANE, split_axis=0, concat_axis=0, tiled=True)

    hidden = pl.pallas_call(
        turn_kernel,
        in_specs=[SMEM, VMEM, ANY, ANY],
        out_specs=VMEM,
        out_shape=struct(REP * YLO * out_rows, Z * rows),
        compiler_params=params(16),
        cost_estimate=cost(0, 2 * 2**20),
        name="turn",
    )(where_at, hidden, near[2], near[-2])
    hidden_other = shift(hidden, "rep", REP, 1)

    half = struct(Z * rows, TEN * HD)
    state = jax.ShapeDtypeStruct(adam_state.shape, adam_state.dtype)
    partial, grads_own, grads_other, state_backup = pl.pallas_call(
        weight_grad_kernel,
        in_specs=[VMEM] * (Z + 3) + [ANY],
        out_specs=[VMEM] * 3 + [HBM],
        out_shape=[struct(YLO, TEN, REP, out_rows, HD), half, half, state],
        scratch_shapes=[pltpu.SemaphoreType.DMA],
        compiler_params=params(32),
        cost_estimate=cost(2 * 2**31, 8 * 2**20),
        name="weight_grad",
    )(hidden, hidden_other, *near, far_up, far_down, state_backup)
    given = pl.pallas_call(
        term_kernel,
        in_specs=[VMEM] * 2,
        out_specs=VMEM,
        out_shape=struct(Z * rows, YLO * w_rows),
        compiler_params=params(24),
        cost_estimate=cost(2**30, 4 * 2**20),
        name="term",
    )(grads_other, weight)
    given = shift(given, "rep", REP, 1)
    partial = partial.reshape(YLO * TEN, REP, out_rows, HD)
    partial = lax.all_to_all(partial, PLANE, split_axis=0, concat_axis=0, tiled=True)

    pieces = pl.pallas_call(
        add_kernel,
        in_specs=[VMEM] * 3,
        out_specs=[VMEM] * Z,
        out_shape=[struct(rows, YLO * w_rows)] * Z,
        compiler_params=params(24),
        cost_estimate=cost(2**30, 5 * 2**20),
        name="add",
    )(grads_own, weight, given)
    moved = {0: pieces[0]}
    for k in (4, 3, 5, 2, 6, 1, 7):
        moved[k] = shift(pieces[k], "z", Z, k)
    moved = [moved[k] for k in range(Z)]
    input_grad = pl.pallas_call(
        join_kernel,
        in_specs=[SMEM] + [VMEM] * Z,
        out_specs=VMEM,
        out_shape=struct(rows, width),
        compiler_params=params(16),
        cost_estimate=cost(0, 2 * 2**20),
        name="join",
    )(where_at, *moved)

    kept, passed = pl.pallas_call(
        sum_kernel,
        in_specs=[SMEM, VMEM] + [ANY] * 3,
        out_specs=[VMEM] * 2,
        out_shape=[struct(out_rows, HD, dtype=F32)] * 2,
        compiler_params=params(16),
        cost_estimate=cost(0, 2 * 2**20),
        name="sum",
    )(where_at, partial, moved[4], moved[3], moved[5])
    passed = shift(passed, "rep", REP, 1)
    key_weight_grad = jnp.where(first, kept, passed)
    value_weight_grad = jnp.where(first, passed, kept)
    return (query_grad, input_grad, key_weight_grad, value_weight_grad, state_backup)


def solution(mesh):
    fine = Mesh(mesh.devices.reshape(REP, YLO, Z, TEN), ("rep", "ylo", "z", "tensor"))
    seqs = ("rep", "ylo", "z")
    return jax.shard_map(
        on_device,
        mesh=fine,
        in_specs=(
            P(seqs + ("tensor",), None),
            P(seqs, "tensor"),
            P(seqs, "tensor"),
            P(seqs, "tensor"),
            P(seqs, "tensor"),
            P(("ylo", "z"), "tensor"),
            P(("ylo", "z"), "tensor"),
            P(None, None, seqs, "tensor"),
        ),
        out_specs=(
            P(seqs, "tensor"),
            P(seqs + ("tensor",), None),
            P(seqs, "tensor"),
            P(seqs, "tensor"),
            P(None, None, seqs, "tensor"),
        ),
        check_vma=False,
    )
```

```python
import math

import jax
import jax.numpy as jnp
import numpy as np
from jax import lax
from jax.experimental import pallas as pl
from jax.experimental.pallas import tpu as pltpu
from jax.sharding import Mesh
from jax.sharding import PartitionSpec as P

HEADS = 64
KVH = 8
HD = 128
GROUP = HEADS // KVH
LEN = 512
REP, YLO, Z, TEN = 2, 2, 8, 8
PLANE = ("ylo", "tensor")
SCALE = 1.0 / math.sqrt(HD)
QB = 256
STEP_HEADS = 4
BF, F32 = jnp.bfloat16, jnp.float32

VMEM = pl.BlockSpec(memory_space=pltpu.VMEM)
SMEM = pl.BlockSpec(memory_space=pltpu.SMEM)
ANY = pl.BlockSpec(memory_space=pl.ANY)
HBM = pl.BlockSpec(memory_space=pltpu.HBM)


def dot(a, b, ca, cb):
    return lax.dot_general(a, b, (((ca,), (cb,)), ((), ())), preferred_element_type=F32)


def struct(*shape, dtype=BF):
    return jax.ShapeDtypeStruct(shape, dtype)


def params(mib):
    return pltpu.CompilerParams(vmem_limit_bytes=mib * 2**20)


def cost(flops, nbytes):
    return pl.CostEstimate(flops=flops, bytes_accessed=nbytes, transcendentals=0)


def shift(block, axis, count, by):
    return lax.ppermute(block, axis, [(i, (i + by) % count) for i in range(count)])


def rope_wide():
    half = HD // 2
    angle = np.arange(LEN)[:, None] * 1000000.0 ** (-2.0 * np.arange(half) / HD)[None, :]
    cosine, sine = np.cos(angle), np.sin(angle)
    wide = np.concatenate([cosine, cosine], 1), np.concatenate([sine, -sine], 1)
    return [jnp.asarray(t.astype(np.float32)) for t in wide]


def attention_kernel(q_ref, k_ref, v_ref, g_ref, c_ref, s_ref, qg_ref, own_ref, other_ref, kt, dk, dv):
    step = pl.program_id(0)

    @pl.when(step == 0)
    def _():
        kt[...] = k_ref[...].T
        dk[...] = jnp.zeros_like(dk)
        dv[...] = jnp.zeros_like(dv)

    key_at = lax.broadcasted_iota(jnp.int32, (QB, QB), 0)
    query_at = lax.broadcasted_iota(jnp.int32, (QB, QB), 1)
    allowed = key_at <= query_at
    for h in range(STEP_HEADS):
        lanes = slice(h * HD, (h + 1) * HD)
        for block in range(LEN // QB):
            rows = slice(block * QB, (block + 1) * QB)
            span = (block + 1) * QB
            q, g = q_ref[rows, lanes], g_ref[rows, lanes]
            scores = dot(k_ref[:span, :], q, 1, 1)
            scores = [scores[i * QB : (i + 1) * QB] for i in range(block + 1)]
            scores[-1] = jnp.where(allowed, scores[-1], -jnp.inf)
            scores = jnp.concatenate(scores, axis=0)
            top = jnp.max(scores, axis=0, keepdims=True)
            weights = jnp.exp2((scores - top) * (SCALE * math.log2(math.e)))
            inverse = 1.0 / jnp.sum(weights, axis=0, keepdims=True)
            probs = weights * inverse
            dprobs = dot(v_ref[:span, :], g, 1, 1)
            delta = jnp.sum(probs * dprobs, axis=0, keepdims=True)
            dscores = (probs * ((dprobs - delta) * SCALE)).astype(BF)
            dk[:span, :] += dot(dscores, q, 1, 0)
            dv[:span, :] += dot(probs.astype(BF), g, 1, 0)
            qg_ref[rows, lanes] = dot(kt[:, :span], dscores, 1, 0).T.astype(BF)

    @pl.when(step == GROUP // STEP_HEADS - 1)
    def _():
        rotated = dk[...]
        turned = pltpu.roll(rotated, HD // 2, 1)
        key_grad = (rotated * c_ref[...] + turned * s_ref[...]).astype(BF)
        value_grad = dv[...].astype(BF)

        rep = lax.axis_index("rep")

        @pl.when(rep == 0)
        def _():
            own_ref[...] = key_grad
            other_ref[...] = value_grad

        @pl.when(rep != 0)
        def _():
            own_ref[...] = value_grad
            other_ref[...] = key_grad


def attention_grads(queries, keys, values, out_grad):
    whole = pl.BlockSpec((LEN, HD), lambda h: (0, 0))
    head = pl.BlockSpec((LEN, STEP_HEADS * HD), lambda h: (0, h))
    return pl.pallas_call(
        attention_kernel,
        grid=(GROUP // STEP_HEADS,),
        in_specs=[head, whole, whole, head, whole, whole],
        out_specs=[head, whole, whole],
        out_shape=[struct(LEN, GROUP * HD), struct(LEN, HD), struct(LEN, HD)],
        scratch_shapes=[
            pltpu.VMEM((HD, LEN), BF),
            pltpu.VMEM((LEN, HD), F32),
            pltpu.VMEM((LEN, HD), F32),
        ],
        compiler_params=params(60),
        cost_estimate=cost(12 * 10**9, 4 * 2**20),
        name="attention_grads",
    )(queries, keys, values, out_grad, *rope_wide())


def deal_kernel(x_ref, out_ref):
    part = out_ref.shape[2] // (REP * YLO)
    for zz in range(Z):
        for i in range(REP * YLO):
            at = (i * Z + zz) * part
            out_ref[zz, :, i * part : (i + 1) * part] = x_ref[:, at : at + part]


def split_kernel(at_ref, own_ref, other_ref, *out_refs):
    ten = at_ref[2]
    rows = out_refs[0].shape[0] // 4
    for k, out_ref in enumerate(out_refs):
        for side in range(2):
            at = pl.multiple_of(lax.bitwise_xor(ten, 2 * k + side) * rows, rows)
            row = 2 * side * rows
            out_ref[row : row + rows, :] = own_ref[pl.ds(at, rows), :]
            out_ref[row + rows : row + 2 * rows, :] = other_ref[pl.ds(at, rows), :]


def middle_kernel(*refs):
    pieces, out_ref = refs[:-1], refs[-1]
    rows = out_ref.shape[1]
    for k, piece in enumerate(pieces):
        out_ref[k] = piece[rows:, :]


def place_kernel(at_ref, *refs):
    pieces, passed_ref, out_ref = refs[: TEN // 2], refs[TEN // 2], refs[-1]
    ten = at_ref[2]
    rows = out_ref.shape[0]
    for k, piece in enumerate(pieces):
        at = pl.multiple_of(lax.bitwise_xor(ten, 2 * k) * HD, HD)
        out_ref[:, pl.ds(at, HD)] = piece[:rows, :]
        at = pl.multiple_of(lax.bitwise_xor(ten, 2 * k + 1) * HD, HD)
        out_ref[:, pl.ds(at, HD)] = passed_ref[k]


def select_kernel(at_ref, key_ref, value_ref, _, out_ref):
    @pl.when(at_ref[0] == 0)
    def _():
        out_ref[...] = key_ref[...]

    @pl.when(at_ref[0] != 0)
    def _():
        out_ref[...] = value_ref[...]


def turn_kernel(at_ref, x_ref, _, __, out_ref):
    z = at_ref[1]
    for j in range(Z // 2):
        one, two = x_ref[lax.rem(z + 2 * j, Z)], x_ref[lax.rem(z + 2 * j + 1, Z)]
        pair = jnp.concatenate([one, two])
        out_ref[:, j * pair.shape[0] : (j + 1) * pair.shape[0]] = pair.T


def side_weight(weight_ref, y, n):
    at = slice(n * 256, (n + 1) * 256)
    return jnp.concatenate([weight_ref[y * TEN + t, at, :] for t in range(TEN)], axis=1)


def term_kernel(grads_ref, weight_ref, out_ref):
    per = weight_ref.shape[1] // 256
    for y in range(YLO):
        for n in range(per):
            at = (y * per + n) * 256
            term = dot(grads_ref[...], side_weight(weight_ref, y, n), 1, 1)
            out_ref[:, at : at + 256] = term.astype(BF)


def add_kernel(grads_ref, weight_ref, given_ref, *outs):
    rows = outs[0].shape[0]
    per = weight_ref.shape[1] // 256
    for y in range(YLO):
        for n in range(per):
            at = (y * per + n) * 256
            term = dot(grads_ref[...], side_weight(weight_ref, y, n), 1, 1)
            term = (term + given_ref[:, at : at + 256].astype(F32)).astype(BF)
            for j, out_ref in enumerate(outs):
                out_ref[:, at : at + 256] = term[j * rows : (j + 1) * rows, :]


def weight_grad_kernel(h_own, h_other, *refs):
    near, (far_up, far_down, state_ref) = refs[: Z - 1], refs[Z - 1 : Z + 2]
    out_ref, own_ref, other_ref, state_out, sem = refs[Z + 2 :]
    rows = far_up.shape[0]
    passing = pltpu.make_async_copy(state_ref, state_out, sem)
    passing.start()
    for j in range(Z):
        at = slice(j * rows, (j + 1) * rows)
        if j == Z // 2:
            own_ref[at, :] = far_up[...]
            other_ref[at, :] = far_down[...]
        else:
            piece = near[j - (j > Z // 2)]
            own_ref[at, :] = piece[:rows, :]
            other_ref[at, :] = piece[rows:, :]
    out_rows = out_ref.shape[3]
    for pair in range(TEN // 2):
        cols = slice(pair * 2 * HD, (pair + 1) * 2 * HD)
        for r in range(REP):
            for y in range(YLO):
                at = slice((r * YLO + y) * out_rows, (r * YLO + y + 1) * out_rows)
                part = dot(h_own[at, :], own_ref[:, cols], 1, 0)
                part = (part + dot(h_other[at, :], other_ref[:, cols], 1, 0)).astype(BF)
                out_ref[y, 2 * pair, r] = part[:, :HD]
                out_ref[y, 2 * pair + 1, r] = part[:, HD:]
    passing.wait()


def sum_kernel(at_ref, x_ref, *refs):
    kept_ref, given_ref = refs[-2:]
    rep = at_ref[0]
    for core, out_ref in ((rep, kept_ref), (1 - rep, given_ref)):
        total = x_ref[0, core].astype(F32)
        for i in range(1, x_ref.shape[0]):
            total = total + x_ref[i, core].astype(F32)
        out_ref[...] = total


def join_kernel(at_ref, *refs):
    *pieces, out_ref, sems = refs
    z = at_ref[1]
    part = pieces[0].shape[1] // YLO
    copies = []
    for s, piece in enumerate(pieces):
        source = lax.rem(z - s + Z, Z)
        for y in range(YLO):
            at = pl.multiple_of((y * Z + source) * part, part)
            copies.append(
                pltpu.make_async_copy(
                    piece.at[:, pl.ds(y * part, part)],
                    out_ref.at[:, pl.ds(at, part)],
                    sems.at[s * YLO + y],
                )
            )
            copies[-1].start()
    for copy in copies:
        copy.wait()


def ring(both):
    rows = both.shape[0] // 2
    up, down = [both], [both]
    for _ in range(Z // 2 - 1):
        up.append(shift(up[-1], "z", Z, 1))
        down.append(shift(down[-1], "z", Z, -1))
    far_up = shift(up[-1][:rows], "z", Z, 1)
    far_down = shift(down[-1][rows:], "z", Z, -1)
    return down + up[:0:-1], far_up, far_down


def on_device(hidden_in, queries, keys, values, out_grad, w_key, w_value, adam_state):
    rep, z, ten = (lax.axis_index(name) for name in ("rep", "z", "tensor"))
    where_at = jnp.stack([rep, z, ten]).astype(jnp.int32)
    first = rep == 0
    state_backup = shift(adam_state, "rep", REP, 1)
    rows, width = hidden_in.shape
    out_rows = width // (REP * YLO * Z)
    w_rows = width // (YLO * Z)

    hidden = pl.pallas_call(
        deal_kernel,
        grid=(2,),
        in_specs=[pl.BlockSpec((rows // 2, width), lambda i: (i, 0))],
        out_specs=pl.BlockSpec((Z, rows // 2, REP * YLO * out_rows), lambda i: (0, i, 0)),
        out_shape=struct(Z, rows, REP * YLO * out_rows),
        compiler_params=params(60),
        cost_estimate=cost(0, 2 * 2**20),
        name="deal",
    )(hidden_in)
    hidden = lax.all_to_all(hidden, "z", split_axis=0, concat_axis=0, tiled=True)

    query_grad, own, other = attention_grads(queries, keys, values, out_grad)
    other = shift(other, "rep", REP, 1)
    pieces = pl.pallas_call(
        split_kernel,
        in_specs=[SMEM, VMEM, VMEM],
        out_specs=[VMEM] * (TEN // 2),
        out_shape=[struct(2 * REP * rows, HD)] * (TEN // 2),
        compiler_params=params(8),
        cost_estimate=cost(0, 2**19),
        name="split",
    )(where_at, own, other)

    def across(block, mask):
        return lax.ppermute(block, "tensor", [(i, i ^ mask) for i in range(TEN)])

    moved = {0: pieces[0]}
    for k in (2, 1, 3):
        moved[k] = across(pieces[k], 2 * k)
    moved = [moved[k] for k in range(TEN // 2)]
    passed = pl.pallas_call(
        middle_kernel,
        in_specs=[VMEM] * (TEN // 2),
        out_specs=VMEM,
        out_shape=struct(TEN // 2, REP * rows, HD),
        compiler_params=params(8),
        cost_estimate=cost(0, 2**18),
        name="middle",
    )(*moved)
    passed = across(passed, 1)
    grads = pl.pallas_call(
        place_kernel,
        in_specs=[SMEM] + [VMEM] * (TEN // 2 + 1) + [ANY],
        out_specs=VMEM,
        out_shape=struct(REP * rows, TEN * HD),
        compiler_params=params(8),
        cost_estimate=cost(0, 2**19),
        name="place",
    )(where_at, *moved, passed, hidden)

    near, far_up, far_down = ring(grads)

    weight = pl.pallas_call(
        select_kernel,
        in_specs=[SMEM, VMEM, VMEM, ANY],
        out_specs=VMEM,
        out_shape=struct(w_rows, HD),
        compiler_params=params(8),
        cost_estimate=cost(0, 2**18),
        name="select",
    )(where_at, w_key, w_value, grads)
    weight = jnp.broadcast_to(weight[None], (YLO * TEN,) + weight.shape)
    weight = lax.all_to_all(weight, PLANE, split_axis=0, concat_axis=0, tiled=True)

    hidden = pl.pallas_call(
        turn_kernel,
        in_specs=[SMEM, VMEM, ANY, ANY],
        out_specs=VMEM,
        out_shape=struct(REP * YLO * out_rows, Z * rows),
        compiler_params=params(16),
        cost_estimate=cost(0, 2 * 2**20),
        name="turn",
    )(where_at, hidden, near[2], near[-2])
    hidden_other = shift(hidden, "rep", REP, 1)

    half = struct(Z * rows, TEN * HD)
    state = jax.ShapeDtypeStruct(adam_state.shape, adam_state.dtype)
    partial, grads_own, grads_other, state_backup = pl.pallas_call(
        weight_grad_kernel,
        in_specs=[VMEM] * (Z + 3) + [ANY],
        out_specs=[VMEM] * 3 + [HBM],
        out_shape=[struct(YLO, TEN, REP, out_rows, HD), half, half, state],
        scratch_shapes=[pltpu.SemaphoreType.DMA],
        compiler_params=params(32),
        cost_estimate=cost(2 * 2**31, 8 * 2**20),
        name="weight_grad",
    )(hidden, hidden_other, *near, far_up, far_down, state_backup)
    given = pl.pallas_call(
        term_kernel,
        in_specs=[VMEM] * 2,
        out_specs=VMEM,
        out_shape=struct(Z * rows, YLO * w_rows),
        compiler_params=params(24),
        cost_estimate=cost(2**30, 4 * 2**20),
        name="term",
    )(grads_other, weight)
    given = shift(given, "rep", REP, 1)
    partial = partial.reshape(YLO * TEN, REP, out_rows, HD)
    partial = lax.all_to_all(partial, PLANE, split_axis=0, concat_axis=0, tiled=True)

    pieces = pl.pallas_call(
        add_kernel,
        in_specs=[VMEM] * 3,
        out_specs=[VMEM] * Z,
        out_shape=[struct(rows, YLO * w_rows)] * Z,
        compiler_params=params(24),
        cost_estimate=cost(2**30, 5 * 2**20),
        name="add",
    )(grads_own, weight, given)
    moved = {0: pieces[0]}
    for k in (4, 3, 5, 2, 6, 1, 7):
        moved[k] = shift(pieces[k], "z", Z, k)
    moved = [moved[k] for k in range(Z)]
    input_grad = pl.pallas_call(
        join_kernel,
        in_specs=[SMEM] + [ANY] * Z,
        out_specs=ANY,
        out_shape=struct(rows, width),
        scratch_shapes=[pltpu.SemaphoreType.DMA((Z * YLO,))],
        compiler_params=params(16),
        cost_estimate=cost(0, 2 * 2**20),
        name="join",
    )(where_at, *moved)

    kept, passed = pl.pallas_call(
        sum_kernel,
        in_specs=[SMEM, VMEM] + [ANY] * 3,
        out_specs=[VMEM] * 2,
        out_shape=[struct(out_rows, HD, dtype=F32)] * 2,
        compiler_params=params(16),
        cost_estimate=cost(0, 2 * 2**20),
        name="sum",
    )(where_at, partial, moved[4], moved[3], moved[5])
    passed = shift(passed, "rep", REP, 1)
    key_weight_grad = jnp.where(first, kept, passed)
    value_weight_grad = jnp.where(first, passed, kept)
    return (query_grad, input_grad, key_weight_grad, value_weight_grad, state_backup)


def solution(mesh):
    fine = Mesh(mesh.devices.reshape(REP, YLO, Z, TEN), ("rep", "ylo", "z", "tensor"))
    seqs = ("rep", "ylo", "z")
    return jax.shard_map(
        on_device,
        mesh=fine,
        in_specs=(
            P(seqs + ("tensor",), None),
            P(seqs, "tensor"),
            P(seqs, "tensor"),
            P(seqs, "tensor"),
            P(seqs, "tensor"),
            P(("ylo", "z"), "tensor"),
            P(("ylo", "z"), "tensor"),
            P(None, None, seqs, "tensor"),
        ),
        out_specs=(
            P(seqs, "tensor"),
            P(seqs + ("tensor",), None),
            P(seqs, "tensor"),
            P(seqs, "tensor"),
            P(None, None, seqs, "tensor"),
        ),
        check_vma=False,
    )
```
